512 devices in a mesh: seq: 32 (over x, z), users: 16 (over y, core).
Axes of the slice: x: 4, y: 8, z: 8, core: 2. Of those that a mesh axis runs over, the one named last changes fastest.
Arguments:
- cand_items: int32 [4096, 2], P(('users', 'seq')), parts along dimension 0, may hold values from 0 to 127
- item_rows: bfloat16 [2048, 1024], P('users'), parts along dimension 0
- hist_keys: bfloat16 [32, 16384, 1024], P('users', 'seq'), parts along dimension 0, may hold values from -6 to 6
- hist_values: bfloat16 [32, 16384, 1024], P('users', 'seq'), parts along dimension 0
- block_mask: int32 [32, 2, 128], P('users', None, 'seq'), parts along dimension 0, may hold values 0 or 1
- hist_lengths: int32 [32], P('users'), parts along dimension 0, may hold values from 4096 to 16384, as said below
- gain_in: float32 [1024], replicated, may hold values from 0.1 to 1.9
- w_query: bfloat16 [1024, 1024], P('seq'), may hold values from -0.1875 to 0.1875
- w_gate: bfloat16 [1024, 1024], P('seq'), may hold values from -0.1875 to 0.1875
- gain_attn: float32 [1024], replicated, may hold values from 0.1 to 1.9
- w_out: bfloat16 [1024, 1024], P('seq'), may hold values from -0.1875 to 0.1875
Outputs:
- ranked: bfloat16 [4096, 2, 1024], P(('users', 'seq')), parts along dimension 0
The draws below stay inside these ranges and needn't reach their ends.
There are 16 independent parts, one for each index of `users`. The reference program is written for one: setup_inputs(seed, part) draws one part's arguments, and reference() takes and returns one part's arrays. A program takes and returns all parts, laid end to end along the dimension named above; an argument that names none is the same for every part. Nothing has to cross between parts.
Inputs may be any that keep to these rules, and one draw needn't show every extreme that they name: `hist_lengths`: in every group at least one user has all 16384 history events valid.
All inputs are finite; a program needn't handle non-finite values. No bound on the sum of `block_mask` on one device may be relied on, other than what follows from the above.
Results may differ from the reference program's by a relative error of at most 0.012.
Values may be sent and summed in bfloat16 or wider, within the bound.
A program may use at most 64 MiB of HBM per device.

```python
import math
import jax
import jax.numpy as jnp
import numpy as np
from jax import lax

HEADS = 8
HEAD_DIM = 128
D = 1024
USERS = 2
CAND = 256
TILE = 128
BLOCK = 128
ITEMS = 128
HIST = 16384
TILES = 2
HBLOCKS = 128


def draw_item_rows(key, part):
    key = jax.random.fold_in(key, 11)
    scale_key, value_key = jax.random.split(key, 2)
    column_scale = jnp.exp(jax.random.uniform(scale_key, (D,), jnp.float32, jnp.log(0.3), jnp.log(3.0)))
    values = jax.random.normal(value_key, (ITEMS, D), jnp.float32)
    return (values * column_scale).astype(jnp.bfloat16)


def draw_hist_values(key, part):
    key = jax.random.fold_in(key, 12)
    scale_key, value_key = jax.random.split(key, 2)
    column_scale = jnp.exp(jax.random.uniform(scale_key, (D,), jnp.float32, jnp.log(0.3), jnp.log(3.0)))
    values = jax.random.normal(value_key, (USERS, HIST, D), jnp.float32)
    return (values * column_scale).astype(jnp.bfloat16)


def draw_hist_lengths(key, part):
    key = jax.random.fold_in(key, 13)
    length_key, choose_key = jax.random.split(key)
    drawn = jax.random.randint(length_key, (USERS,), HIST // 4, HIST + 1, dtype=jnp.int32)
    full_user = jax.random.randint(choose_key, (), 0, USERS, dtype=jnp.int32)
    return jnp.where(jnp.arange(USERS, dtype=jnp.int32) == full_user, HIST, drawn).astype(jnp.int32)


def with_ends(values, rng, smallest, high):
    extent = values.shape
    place = [jax.random.randint(jax.random.fold_in(rng, axis), (), 0, extent[axis]) for axis in range(len(extent))]
    values = values.at[tuple(place)].set(smallest)
    longest = extent.index(max(extent))
    place[longest] = (place[longest] + 1) % extent[longest]
    return values.at[tuple(place)].set(high)


def shard_levels(rng, dims, cuts, least, top_value):
    def one(axis_at, parts):
        draws = jax.random.uniform(jax.random.fold_in(jax.random.fold_in(rng, 6), axis_at), (parts,), jnp.float32, least / len(cuts), top_value / len(cuts))
        return jnp.repeat(jnp.exp(draws), dims[axis_at] // parts).reshape((-1,) + (1,) * (len(dims) - axis_at - 1))

    level = one(*cuts[0])
    for cut in cuts[1:]:
        level = level * one(*cut)
    return level


def cumulative_ranks(amount, skew):
    weights = [(1 << 20) // math.isqrt(standing ** skew) + 1 for standing in range(1, amount + 1)]
    spread = 1 + sum(weights) // (1 << 30)
    return np.cumsum(np.array([max(1, weight // spread) for weight in weights]))


def ranked(own_key, dims, number_of, slope):
    listing = cumulative_ranks(number_of, slope)
    ticket = jax.random.randint(jax.random.fold_in(own_key, 1), dims, 0, int(listing[number_of - 1]))
    standing = jnp.searchsorted(jnp.asarray(listing, jnp.int32), ticket, side="right")
    return jax.random.permutation(jax.random.fold_in(own_key, 2), number_of)[standing].astype(jnp.int32)


def normal_values(rng, extent, width, bound, cuts=(), kind=jnp.bfloat16):
    result = width * jax.random.normal(rng, extent, jnp.float32)
    if cuts:
        result = result * shard_levels(rng, extent, cuts, -0.22, 0.18)
    return jnp.clip(result, -bound, bound).astype(kind)


def setup_inputs(seed: int = 0, part: int = 0) -> dict:
    key_of = jax.random.split(jax.random.key(seed), 12)
    part_splits = jax.random.split(jax.random.fold_in(key_of[11], part), 12)
    cand_items = with_ends(ranked(part_splits[0], (CAND, USERS), ITEMS, 2), jax.random.fold_in(part_splits[0], 3), 0, ITEMS - 1).astype(jnp.int32)
    item_rows = draw_item_rows(jax.random.fold_in(jax.random.fold_in(key_of[11], part), 71), part)
    hist_keys = normal_values(part_splits[2], (USERS, HIST, D), 1.0, 6.0, ((1, 32),))
    hist_values = draw_hist_values(jax.random.fold_in(jax.random.fold_in(key_of[11], part), 71), part)
    block_mask = with_ends((jax.random.randint(part_splits[4], (USERS, TILES, HBLOCKS), 0, 2) < 1).astype(jnp.int32), jax.random.fold_in(part_splits[4], 1), 0, 1)
    hist_lengths = draw_hist_lengths(jax.random.fold_in(jax.random.fold_in(key_of[11], part), 71), part)
    gain_in = jnp.clip(1.0 + 0.18 * jax.random.normal(key_of[6], (D,), jnp.float32), 0.1, 1.9)
    w_query = normal_values(key_of[7], (D, D), D ** -0.5, 0.1875, ((0, 32),))
    w_gate = normal_values(key_of[8], (D, D), D ** -0.5, 0.1875, ((0, 32),))
    gain_attn = jnp.clip(1.0 + 0.18 * jax.random.normal(key_of[9], (D,), jnp.float32), 0.1, 1.9)
    w_out = normal_values(key_of[10], (D, D), D ** -0.5, 0.1875, ((0, 32),))
    return {"cand_items": cand_items, "item_rows": item_rows, "hist_keys": hist_keys, "hist_values": hist_values, "block_mask": block_mask, "hist_lengths": hist_lengths, "gain_in": gain_in, "w_query": w_query, "w_gate": w_gate, "gain_attn": gain_attn, "w_out": w_out}


EPSILON = 1e-06

def scaled_rows(values, gain):
    wide = values.astype(jnp.float32)
    return wide * lax.rsqrt(lax.optimization_barrier(jnp.mean(wide * wide, axis=-1, keepdims=True)) + EPSILON) * gain

def reference(cand_items, item_rows, hist_keys, hist_values, block_mask, hist_lengths, gain_in, w_query, w_gate, gain_attn, w_out):
    tokens = item_rows[cand_items]
    flat = scaled_rows(tokens, gain_in).astype(jnp.bfloat16).reshape(CAND * USERS, D)
    query = jax.nn.silu(jnp.dot(flat, w_query, preferred_element_type=jnp.float32)).astype(jnp.bfloat16)
    query = query.reshape(CAND, USERS, HEADS, HEAD_DIM)
    gate = jax.nn.silu(jnp.dot(flat, w_gate, preferred_element_type=jnp.float32)).astype(jnp.bfloat16)
    gate = gate.reshape(CAND, USERS, D)
    score_scale = HEAD_DIM ** (-0.5)
    tile_of = jnp.arange(CAND, dtype=jnp.int32) // TILE
    results = []
    for user_index in range(USERS):
        queries = query[:, user_index].astype(jnp.float32)
        keys_all = hist_keys[user_index].reshape(HBLOCKS, BLOCK, HEADS, HEAD_DIM)
        values_all = hist_values[user_index].reshape(HBLOCKS, BLOCK, HEADS, HEAD_DIM)
        mask_rows = block_mask[user_index][tile_of]
        length = hist_lengths[user_index]

        def one_block(running, operands):
            keys_block, values_block, open_rows, block_index = operands
            scores = jnp.einsum('chd,ehd->hce', queries, keys_block.astype(jnp.float32)) * score_scale
            positions = block_index * BLOCK + jnp.arange(BLOCK, dtype=jnp.int32)
            keep = (open_rows == 1)[:, None] & (positions < length)[None, :]
            weights = jnp.where(keep[None], jax.nn.silu(scores), 0.0).astype(jnp.bfloat16)
            update = jnp.einsum('hce,ehd->chd', weights.astype(jnp.float32), values_block.astype(jnp.float32))
            return (running + update, None)
        start_sum = jnp.zeros((CAND, HEADS, HEAD_DIM), jnp.float32)
        final_sum, unused = lax.scan(one_block, start_sum, (keys_all, values_all, mask_rows.T, jnp.arange(HBLOCKS, dtype=jnp.int32)))
        results.append(final_sum.reshape(CAND, D))
    attended = jnp.stack(results, axis=1)
    mixed = (scaled_rows(attended, gain_attn) * gate.astype(jnp.float32)).astype(jnp.bfloat16)
    projected = jnp.dot(mixed.reshape(CAND * USERS, D), w_out, preferred_element_type=jnp.float32)
    return (tokens.astype(jnp.float32) + projected.reshape(CAND, USERS, D)).astype(jnp.bfloat16)
```

```python
import jax
import jax.numpy as jnp
from jax import lax
from jax.experimental import pallas as pl
from jax.experimental.pallas import tpu as pltpu
from jax.sharding import PartitionSpec as P

HEADS = 8
HEAD_DIM = 128
BLOCK = 128
EPSILON = 1e-06
XS, ZS = 4, 8
NEAREST = (7, 1, 6, 2, 5, 3, 4)
MESH = pl.DeviceIdType.MESH
BF16, F32 = jnp.bfloat16, jnp.float32


def silu(v):
    return v / (1.0 + jnp.exp(-v))


def push(src, dst, send_sem, recv_sem, seq):
    return pltpu.make_async_remote_copy(
        src_ref=src, dst_ref=dst, send_sem=send_sem, recv_sem=recv_sem,
        device_id={"seq": seq}, device_id_type=MESH)


def kernel(
    cand, items_hbm, keys_hbm, vals_hbm, mask, lens, gain_in, wq_hbm, wg_hbm, gain_attn, wo_hbm,
    out,
    items, keys, vals, normed, picks, ids_x, chooser, live, tokens, wq, wg, wo_rows, wo, query, gate,
    part, part_in, half, half_in, proj, proj_in, sq, sq_in,
    load_sem, wq_zs, wq_zr, wq_xs, wq_xr, wg_zs, wg_zr, wg_xs, wg_xr, oh_zs, oh_zr, oh_xs, oh_xr,
    wo_xs, wo_xr, wo_zs, wo_zr, q_s, q_r, rx_s, rx_r, rz_s, rz_r, po_s, po_r, sq_s, sq_r,
):
    me = lax.axis_index("seq")
    x, z = lax.div(me, ZS), lax.rem(me, ZS)
    rows = wq_hbm.shape[0]
    own = picks.shape[1]
    users, events = keys_hbm.shape[0], keys_hbm.shape[1]
    item_count = items_hbm.shape[0]

    def z_at(step):
        return lax.rem(z + step + ZS, ZS)

    def x_at(step):
        return lax.rem(x + step + XS, XS)

    def lanes(index):
        return pl.ds(pl.multiple_of(index * HEAD_DIM, HEAD_DIM), HEAD_DIM)

    def rows_of(seq):
        return pl.ds(pl.multiple_of(seq * rows, rows), rows)

    barrier = pltpu.get_barrier_semaphore()
    for j in range(1, ZS):
        pl.semaphore_signal(barrier, inc=1, device_id={"seq": x * ZS + z_at(j)}, device_id_type=MESH)
    for j in range(1, XS):
        pl.semaphore_signal(barrier, inc=1, device_id={"seq": x_at(j) * ZS + z}, device_id_type=MESH)

    loads = [
        pltpu.make_async_copy(items_hbm, items, load_sem.at[0]),
        pltpu.make_async_copy(wq_hbm.at[:, lanes(z)], wq.at[rows_of(me)], load_sem.at[1]),
        pltpu.make_async_copy(wg_hbm.at[:, lanes(z)], wg.at[rows_of(me)], load_sem.at[2]),
        pltpu.make_async_copy(wo_hbm, wo_rows.at[x], load_sem.at[3]),
    ]
    for u in range(users):
        loads.append(pltpu.make_async_copy(keys_hbm.at[u], keys.at[u], load_sem.at[4 + 2 * u]))
        loads.append(pltpu.make_async_copy(vals_hbm.at[u], vals.at[u], load_sem.at[5 + 2 * u]))
    for load in loads:
        load.start()

    row = lax.broadcasted_iota(jnp.int32, (own, own // users), 0)
    column = lax.broadcasted_iota(jnp.int32, (own, own // users), 1)
    ids = jnp.zeros((own, 1), F32)
    for u in range(users):
        here = row == column * users + u
        ids += jnp.sum(
            jnp.where(here, cand[u : u + 1, :].astype(F32), 0.0), axis=1, keepdims=True)
    item = lax.broadcasted_iota(jnp.int32, (own, item_count), 1).astype(F32)
    own_pick = jnp.where(item == ids, 1.0, 0.0).astype(BF16)
    picks[z] = own_pick

    pl.semaphore_wait(barrier, XS + ZS - 2)

    sends = []

    def send(copy):
        copy.start()
        sends.append(copy)

    for j in range(1, ZS):
        to = z_at(j)
        send(push(wq_hbm.at[:, lanes(to)], wq.at[rows_of(me)], wq_zs.at[j], wq_zr.at[j], x * ZS + to))
    for j in range(1, XS):
        send(push(wo_hbm, wo_rows.at[x], wo_xs.at[j], wo_xr.at[j], x_at(j) * ZS + z))

    loads[0].wait()
    wide = items[...].astype(F32)
    normed[...] = (
        wide * lax.rsqrt(jnp.mean(wide * wide, axis=-1, keepdims=True) + EPSILON) * gain_in[...]
    ).astype(BF16)

    def group(at):
        return pl.ds(pl.multiple_of(at * (ZS * rows), ZS * rows), ZS * rows)

    def widen(buf, zr, xs, xr):
        for j in range(1, ZS):
            come = buf.at[rows_of(x * ZS + z_at(-j))]
            push(come, come, zr.at[j], zr.at[j], me).wait_recv()
        for j in range(1, XS):
            send(push(buf.at[group(x)], buf.at[group(x)], xs.at[j], xr.at[j], x_at(j) * ZS + z))

    loads[1].wait()
    widen(wq, wq_zr, wq_xs, wq_xr)

    for j in range(1, ZS):
        to = z_at(j)
        send(push(picks.at[z], picks.at[z], oh_zs.at[j], oh_zr.at[j], x * ZS + to))
    for j in range(1, ZS):
        to = z_at(j)
        send(push(wg_hbm.at[:, lanes(to)], wg.at[rows_of(me)], wg_zs.at[j], wg_zr.at[j], x * ZS + to))

    tokens[...] = jnp.dot(own_pick, items[...], preferred_element_type=F32)
    tiles = mask.shape[1]
    for u in range(users):
        length = lens[u] - me * events
        for t in range(tiles):
            for b in range(events // BLOCK):
                place = b * BLOCK + lax.broadcasted_iota(jnp.int32, (1, BLOCK), 1)
                opened = jnp.full((1, BLOCK), mask[u, t, b], jnp.int32)
                live[pl.ds(u * tiles + t, 1), pl.ds(b * BLOCK, BLOCK)] = jnp.where(
                    (opened == 1) & (place < length), 1.0, 0.0)

    for j in range(1, XS):
        come = wq.at[group(x_at(-j))]
        push(come, come, wq_xr.at[j], wq_xr.at[j], me).wait_recv()
    query[z] = silu(jnp.dot(normed[...], wq[...], preferred_element_type=F32)).astype(BF16)
    for j in NEAREST:
        send(push(query.at[z], query.at[z], q_s.at[j], q_r.at[j], x * ZS + z_at(j)))

    for j in range(1, ZS):
        come = picks.at[z_at(-j)]
        push(come, come, oh_zr.at[j], oh_zr.at[j], me).wait_recv()
    group_rows = ZS * own
    picked = picks[...].reshape(group_rows, item_count)
    number = lax.broadcasted_iota(jnp.int32, (own, item_count), 1).astype(F32).astype(BF16)
    ids_x[x] = lax.dot_general(
        number, picked, (((1,), (1,)), ((), ())), preferred_element_type=F32).astype(BF16)
    for j in range(1, XS):
        send(push(ids_x.at[x], ids_x.at[x], oh_xs.at[j], oh_xr.at[j], x_at(j) * ZS + z))

    loads[2].wait()
    widen(wg, wg_zr, wg_xs, wg_xr)

    for j in range(1, XS):
        come = ids_x.at[x_at(-j)]
        push(come, come, oh_xr.at[j], oh_xr.at[j], me).wait_recv()
    user_of = lax.rem(lax.broadcasted_iota(jnp.int32, (group_rows, item_count), 0), users)
    down = lax.broadcasted_iota(jnp.int32, (item_count, group_rows), 0).astype(F32)
    per_tile = XS // tiles
    for s in range(XS):
        chosen = jnp.transpose(jnp.where(down == ids_x[s, 0:1, :].astype(F32), 1.0, 0.0))
        for u in range(users):
            chooser[s // per_tile, pl.ds(s % per_tile * group_rows, group_rows),
                    pl.ds(u * item_count, item_count)] = jnp.where(
                        user_of == u, chosen, 0.0).astype(BF16)

    per_head = HEAD_DIM // rows
    slot = lax.rem(z, per_head)
    place_wo = pl.ds(pl.multiple_of(slot * rows, rows), rows)
    heads_x = ZS // per_head

    def spread_wo():
        for j in range(1, XS):
            come = wo_rows.at[x_at(-j)]
            push(come, come, wo_xr.at[j], wo_xr.at[j], me).wait_recv()
        loads[3].wait()
        for s in range(XS):
            to = s * heads_x + lax.div(z, per_head)
            copy = push(wo_rows.at[s], wo.at[place_wo], wo_zs.at[s], wo_zr.at[slot], x * ZS + to)

            @pl.when(to != z)
            def _():
                copy.start()

            @pl.when(to == z)
            def _():
                wo[place_wo] = wo_rows[s]

    def make_gate():
        for j in range(1, XS):
            come = wg.at[group(x_at(-j))]
            push(come, come, wg_xr.at[j], wg_xr.at[j], me).wait_recv()
        gate_items = silu(jnp.dot(normed[...], wg[...], preferred_element_type=F32)).astype(BF16)
        rows_x = picks[...].reshape(group_rows, item_count)
        gate[...] = jnp.dot(rows_x, gate_items, preferred_element_type=F32) * gain_attn[:, lanes(z)]

    for load in loads[4:]:
        load.wait()

    lag = 2

    def head_of(k):
        flip = 1 - 2 * lax.rem(k + 1, 2)
        return lax.rem(z + flip * lax.div(k + 1, 2) + ZS, ZS)

    def attend(k):
        h = head_of(k)
        j = lax.rem(z - h + ZS, ZS)

        @pl.when(k > 0)
        def _():
            push(query.at[h], query.at[h], q_r.at[j], q_r.at[j], me).wait_recv()

        asked = query[h]
        sums = []
        for u in range(users):
            scores = lax.dot_general(
                asked, keys[u, :, lanes(h)], (((1,), (1,)), ((), ())), preferred_element_type=F32)
            halved = scores * (0.5 * HEAD_DIM ** (-0.5))
            weight = halved + halved * jnp.tanh(halved)
            kept = jnp.concatenate(
                [weight * live[pl.ds(u * tiles + t, 1), :] for t in range(tiles)], axis=0)
            sums.append(jnp.dot(
                kept.astype(BF16), vals[u, :, lanes(h)], preferred_element_type=F32).astype(BF16))
        for t in range(tiles):
            both = jnp.concatenate(
                [s[t * item_count : (t + 1) * item_count] for s in sums], axis=0)
            sel = jnp.dot(chooser[t], both, preferred_element_type=F32).astype(BF16)
            for i in range(XS // tiles):
                part[h, t * (XS // tiles) + i] = sel[i * group_rows : (i + 1) * group_rows]
        for j in range(1, XS):
            to = x_at(j)
            push(part.at[h, to], part_in.at[h, x], rx_s.at[k * XS + j], rx_r.at[k * XS + j],
                 to * ZS + z).start()

    def reduce_x(k):
        h = head_of(k)
        total = part[h, x].astype(F32)
        for j in range(1, XS):
            come = part_in.at[h, x_at(-j)]
            push(come, come, rx_r.at[k * XS + j], rx_r.at[k * XS + j], me).wait_recv()
            total += part_in[h, x_at(-j)].astype(F32)
        half[h] = total.astype(BF16)

        @pl.when(k > 0)
        def _():
            j = lax.rem(h - z + ZS, ZS)
            push(half.at[h], half_in.at[z], rz_s.at[j], rz_r.at[j], x * ZS + h).start()

    def step(k, carry):
        @pl.when(k < HEADS)
        def _():
            attend(k)

        @pl.when(k == HEADS // 2)
        def _():
            spread_wo()

        @pl.when(k == HEADS)
        def _():
            make_gate()

        @pl.when(k >= lag)
        def _():
            reduce_x(k - lag)

        return carry

    lax.fori_loop(0, HEADS + lag, step, 0)

    for i in range(per_head):
        frm = per_head * lax.rem(z, heads_x) + i

        @pl.when(frm != z)
        def _():
            come = wo.at[pl.ds(i * rows, rows)]
            push(come, come, wo_zr.at[i], wo_zr.at[i], me).wait_recv()

    attended = half[z].astype(F32)
    for j in range(1, ZS):
        come = half_in.at[z_at(-j)]
        push(come, come, rz_r.at[j], rz_r.at[j], me).wait_recv()
        attended += half_in[z_at(-j)].astype(F32)
    sq[...] = (attended * attended).reshape(sq.shape)
    for j in range(1, ZS):
        to = z_at(j)
        send(push(sq.at[to], sq_in.at[z], sq_s.at[j], sq_r.at[j], x * ZS + to))
    proj[...] = jnp.dot(
        (attended * gate[...]).astype(BF16), wo[...], preferred_element_type=F32
    ).astype(BF16).reshape(proj.shape)
    for j in range(1, ZS):
        to = z_at(j)
        send(push(proj.at[to], proj_in.at[z], po_s.at[j], po_r.at[j], x * ZS + to))

    squares = sq[z]
    for j in range(1, ZS):
        come = sq_in.at[z_at(-j)]
        push(come, come, sq_r.at[j], sq_r.at[j], me).wait_recv()
        squares += sq_in[z_at(-j)]
    scale = lax.rsqrt(jnp.sum(squares, axis=1, keepdims=True) * (1.0 / (HEADS * HEAD_DIM)) + EPSILON)
    projected = proj[z].astype(F32)
    for j in range(1, ZS):
        come = proj_in.at[z_at(-j)]
        push(come, come, po_r.at[j], po_r.at[j], me).wait_recv()
        projected += proj_in[z_at(-j)].astype(F32)
    out[...] = (tokens[...] + projected * scale).astype(BF16)

    for copy in sends:
        copy.wait_send()
    for s in range(XS):
        to = s * heads_x + lax.div(z, per_head)

        @pl.when(to != z)
        def _():
            push(wo_rows.at[s], wo.at[place_wo], wo_zs.at[s], wo_zr.at[slot], x * ZS + to).wait_send()

    def drain(k, carry):
        for j in range(1, XS):
            gone = part.at[head_of(k), x_at(j)]
            push(gone, gone, rx_s.at[k * XS + j], rx_r.at[k * XS + j], me).wait_send()
        return carry

    lax.fori_loop(0, HEADS, drain, 0)
    for j in range(1, ZS):
        gone = half.at[z_at(j)]
        push(gone, gone, rz_s.at[j], rz_r.at[j], me).wait_send()


def on_device(
    cand_items, item_rows, hist_keys, hist_values, block_mask, hist_lengths,
    gain_in, w_query, w_gate, gain_attn, w_out,
):
    row_count, users = cand_items.shape
    item_count, width = item_rows.shape
    events = hist_keys.shape[1]
    rows = w_query.shape[0]
    own = row_count * users
    tiles = block_mask.shape[1]
    group_rows = ZS * own
    dma = pltpu.SemaphoreType.DMA
    anywhere = pl.BlockSpec(memory_space=pl.ANY)
    vmem = pl.BlockSpec(memory_space=pltpu.VMEM)
    smem = pl.BlockSpec(memory_space=pltpu.SMEM)
    ranked = pl.pallas_call(
        kernel,
        out_shape=jax.ShapeDtypeStruct((own, width), BF16),
        in_specs=[vmem, anywhere, anywhere, anywhere, smem, smem, vmem, anywhere, anywhere, vmem, anywhere],
        out_specs=vmem,
        scratch_shapes=[
            pltpu.VMEM((item_count, width), BF16),
            pltpu.VMEM((users, events, width), BF16),
            pltpu.VMEM((users, events, width), BF16),
            pltpu.VMEM((item_count, width), BF16),
            pltpu.VMEM((ZS, own, item_count), BF16),
            pltpu.VMEM((XS, own, group_rows), BF16),
            pltpu.VMEM((tiles, XS * ZS // tiles * own, users * item_count), BF16),
            pltpu.VMEM((users * tiles, events), F32),
            pltpu.VMEM((own, width), F32),
            pltpu.VMEM((XS * ZS * rows, HEAD_DIM), BF16),
            pltpu.VMEM((XS * ZS * rows, HEAD_DIM), BF16),
            pltpu.VMEM((XS, rows, width), BF16),
            pltpu.VMEM((HEAD_DIM, width), BF16),
            pltpu.VMEM((HEADS, item_count, HEAD_DIM), BF16),
            pltpu.VMEM((group_rows, HEAD_DIM), F32),
            pltpu.VMEM((HEADS, XS, group_rows, HEAD_DIM), BF16),
            pltpu.VMEM((HEADS, XS, group_rows, HEAD_DIM), BF16),
            pltpu.VMEM((HEADS, group_rows, HEAD_DIM), BF16),
            pltpu.VMEM((ZS, group_rows, HEAD_DIM), BF16),
            pltpu.VMEM((ZS, own, width), BF16),
            pltpu.VMEM((ZS, own, width), BF16),
            pltpu.VMEM((ZS, own, HEAD_DIM), F32),
            pltpu.VMEM((ZS, own, HEAD_DIM), F32),
            dma((4 + 2 * users,)),
            dma((ZS,)), dma((ZS,)), dma((XS,)), dma((XS,)),
            dma((ZS,)), dma((ZS,)), dma((XS,)), dma((XS,)),
            dma((ZS,)), dma((ZS,)), dma((XS,)), dma((XS,)),
            dma((XS,)), dma((XS,)), dma((XS,)), dma((HEAD_DIM // rows,)),
            dma((ZS,)), dma((ZS,)),
            dma((HEADS * XS,)), dma((HEADS * XS,)),
            dma((ZS,)), dma((ZS,)),
            dma((ZS,)), dma((ZS,)),
            dma((ZS,)), dma((ZS,)),
        ],
        compiler_params=pltpu.CompilerParams(
            collective_id=0, has_side_effects=True, vmem_limit_bytes=63 * 1024 * 1024),
        cost_estimate=pl.CostEstimate(flops=10**9, bytes_accessed=5 * 10**6, transcendentals=10**6),
        name="ranked",
    )(
        cand_items.T, item_rows, hist_keys, hist_values, block_mask, hist_lengths,
        gain_in.reshape(1, width), w_query, w_gate, gain_attn.reshape(1, width), w_out,
    )
    return ranked.reshape(row_count, users, width)


def solution(mesh):
    in_specs = (
        P(("users", "seq"), None),
        P("users", None),
        P("users", "seq", None),
        P("users", "seq", None),
        P("users", None, "seq"),
        P("users"),
        P(),
        P("seq", None),
        P("seq", None),
        P(),
        P("seq", None),
    )
    out_specs = P(("users", "seq"), None, None)
    return jax.shard_map(
        on_device, mesh=mesh, in_specs=in_specs, out_specs=out_specs, check_vma=False
    )
```

```python
import jax
import jax.numpy as jnp
from jax import lax
from jax.experimental import pallas as pl
from jax.experimental.pallas import tpu as pltpu
from jax.sharding import PartitionSpec as P

HEADS = 8
HEAD_DIM = 128
BLOCK = 128
EPSILON = 1e-06
XS, ZS = 4, 8
NEAREST = (7, 1, 6, 2, 5, 3, 4)
TEAM = 4
MESH = pl.DeviceIdType.MESH
BF16, F32 = jnp.bfloat16, jnp.float32


def silu(v):
    return v / (1.0 + jnp.exp(-v))


def push(src, dst, send_sem, recv_sem, seq):
    return pltpu.make_async_remote_copy(
        src_ref=src, dst_ref=dst, send_sem=send_sem, recv_sem=recv_sem,
        device_id={"seq": seq}, device_id_type=MESH)


def kernel(
    cand_hbm, items_hbm, keys_hbm, vals_hbm, mask_hbm, lens_hbm, gain_in_hbm, wq_hbm, wg_hbm,
    gain_attn_hbm, wo_hbm,
    out,
    cand, mask, lens, gain_in, gain_attn, items, keys, vals, normed, picks, ids_x, chooser, live,
    tokens, wq, wg, wo, query, gate_out, gate_in, part, part_in, half, half_in, proj, proj_in, sq, sq_in,
    load_sem, wq_zs, wq_zr, wq_xs, wq_xr, wg_zs, wg_zr, wg_xs, wg_xr, oh_zs, oh_zr, oh_xs, oh_xr,
    wo_zs, wo_zr, wo_ts, wo_tr, q_s, q_r, ga_s, ga_r, rx_s, rx_r, rz_s, rz_r, po_s, po_r, sq_s, sq_r,
):
    me = lax.axis_index("seq")
    x, z = lax.div(me, ZS), lax.rem(me, ZS)
    team = min(TEAM, lax.axis_size("users"))
    member = lax.rem(lax.axis_index("users"), team)
    team_at = lax.axis_index("users") - member
    rows = wq_hbm.shape[0]
    own = picks.shape[1]
    tiles = mask.shape[1]
    users, events = keys_hbm.shape[0], keys_hbm.shape[1]
    item_count = items_hbm.shape[0]

    def z_at(step):
        return lax.rem(z + step + ZS, ZS)

    def x_at(step):
        return lax.rem(x + step + XS, XS)

    def lanes(index):
        return pl.ds(pl.multiple_of(index * HEAD_DIM, HEAD_DIM), HEAD_DIM)

    def rows_of(seq):
        return pl.ds(pl.multiple_of(seq * rows, rows), rows)

    share = wo_hbm.shape[1] // team

    def share_of(at):
        return pl.ds(pl.multiple_of(at * share, share), share)

    def mate(step):
        return lax.rem(member + step, team)

    barrier = pltpu.get_barrier_semaphore()
    for j in range(1, ZS):
        pl.semaphore_signal(barrier, inc=1, device_id={"seq": x * ZS + z_at(j)}, device_id_type=MESH)
    for j in range(1, XS):
        pl.semaphore_signal(barrier, inc=1, device_id={"seq": x_at(j) * ZS + z}, device_id_type=MESH)

    for j in range(1, team):
        pl.semaphore_signal(barrier, inc=1, device_id={"users": team_at + mate(j)}, device_id_type=MESH)

    loads = [
        pltpu.make_async_copy(cand_hbm, cand, load_sem.at[0]),
        pltpu.make_async_copy(items_hbm, items, load_sem.at[1]),
        pltpu.make_async_copy(gain_in_hbm, gain_in, load_sem.at[2]),
        pltpu.make_async_copy(wq_hbm.at[:, lanes(z)], wq.at[rows_of(me)], load_sem.at[3]),
        pltpu.make_async_copy(wg_hbm.at[:, lanes(z)], wg.at[rows_of(me)], load_sem.at[4]),
        pltpu.make_async_copy(
            wo_hbm.at[:, share_of(member)], wo.at[rows_of(z), share_of(member)], load_sem.at[5]),
        pltpu.make_async_copy(gain_attn_hbm, gain_attn, load_sem.at[6]),
        pltpu.make_async_copy(mask_hbm, mask, load_sem.at[7]),
        pltpu.make_async_copy(lens_hbm, lens, load_sem.at[8]),
    ]
    for u in range(users):
        loads.append(pltpu.make_async_copy(keys_hbm.at[u], keys.at[u], load_sem.at[9 + 2 * u]))
        loads.append(pltpu.make_async_copy(vals_hbm.at[u], vals.at[u], load_sem.at[10 + 2 * u]))
    for load in loads[:4]:
        load.start()

    pl.semaphore_wait(barrier, XS + ZS + team - 3)

    sends = []

    def send(copy):
        copy.start()
        sends.append(copy)

    for j in range(1, ZS):
        to = z_at(j)
        send(push(wq_hbm.at[:, lanes(to)], wq.at[rows_of(me)], wq_zs.at[j], wq_zr.at[j], x * ZS + to))
    for load in loads[4:]:
        load.start()

    loads[0].wait()
    each = own // users
    row = lax.broadcasted_iota(jnp.int32, (own, each), 0)
    column = lax.broadcasted_iota(jnp.int32, (own, each), 1)
    ids = jnp.zeros((own, 1), F32)
    for u in range(users):
        here = row == column + u * each
        ids += jnp.sum(
            jnp.where(here, cand[u : u + 1, :].astype(F32), 0.0), axis=1, keepdims=True)
    item = lax.broadcasted_iota(jnp.int32, (own, item_count), 1).astype(F32)
    own_pick = jnp.where(item == ids, 1.0, 0.0).astype(BF16)
    picks[z] = own_pick

    for j in range(1, ZS):
        send(push(picks.at[z], picks.at[z], oh_zs.at[j], oh_zr.at[j], x * ZS + z_at(j)))

    loads[1].wait()
    loads[2].wait()
    wide = items[...].astype(F32)
    normed[...] = (
        wide * lax.rsqrt(jnp.mean(wide * wide, axis=-1, keepdims=True) + EPSILON) * gain_in[...]
    ).astype(BF16)

    def group(at):
        return pl.ds(pl.multiple_of(at * (ZS * rows), ZS * rows), ZS * rows)

    loads[3].wait()
    for j in range(1, ZS):
        come = wq.at[rows_of(x * ZS + z_at(-j))]
        push(come, come, wq_zr.at[j], wq_zr.at[j], me).wait_recv()
    for j in range(1, XS):
        send(push(wq.at[group(x)], wq.at[group(x)], wq_xs.at[j], wq_xr.at[j], x_at(j) * ZS + z))

    for j in range(1, ZS):
        to = z_at(j)
        send(push(wg_hbm.at[:, lanes(to)], wg.at[rows_of(me)], wg_zs.at[j], wg_zr.at[j], x * ZS + to))

    for j in range(1, ZS):
        come = picks.at[z_at(-j)]
        push(come, come, oh_zr.at[j], oh_zr.at[j], me).wait_recv()
    group_rows = ZS * own
    picked = picks[...].reshape(group_rows, item_count)
    number = lax.broadcasted_iota(jnp.int32, (own, item_count), 1).astype(F32).astype(BF16)
    ids_x[x] = lax.dot_general(
        number, picked, (((1,), (1,)), ((), ())), preferred_element_type=F32).astype(BF16)
    for j in range(1, XS):
        send(push(ids_x.at[x], ids_x.at[x], oh_xs.at[j], oh_xr.at[j], x_at(j) * ZS + z))

    tokens[...] = jnp.dot(own_pick, items[...], preferred_element_type=F32)
    loads[7].wait()
    loads[8].wait()
    for u in range(users):
        length = lens[u] - me * events
        for t in range(tiles):
            for b in range(events // BLOCK):
                place = b * BLOCK + lax.broadcasted_iota(jnp.int32, (1, BLOCK), 1)
                opened = jnp.full((1, BLOCK), mask[u, t, b], jnp.int32)
                live[u * tiles + t, :, pl.ds(b * BLOCK, BLOCK)] = jnp.where(
                    (opened == 1) & (place < length), 1.0, 0.0)

    for j in range(1, XS):
        come = wq.at[group(x_at(-j))]
        push(come, come, wq_xr.at[j], wq_xr.at[j], me).wait_recv()
    query[z] = silu(jnp.dot(normed[...], wq[...], preferred_element_type=F32)).astype(BF16)
    for j in NEAREST:
        send(push(query.at[z], query.at[z], q_s.at[j], q_r.at[j], x * ZS + z_at(j)))

    gate_x = lax.div(z, HEADS // XS)
    gate_step = lax.rem(gate_x - x + XS, XS)
    wg_copy = push(wg.at[group(x)], wg.at[group(x)], wg_xs.at[gate_step], wg_xr.at[gate_step],
                   gate_x * ZS + z)
    slot = lax.rem(z, HEADS // XS)
    loads[4].wait()
    for j in range(1, ZS):
        come = wg.at[rows_of(x * ZS + z_at(-j))]
        push(come, come, wg_zr.at[j], wg_zr.at[j], me).wait_recv()

    @pl.when(gate_x != x)
    def _():
        wg_copy.start()

    for j in range(1, ZS):
        send(push(wo_hbm.at[:, share_of(member)], wo.at[rows_of(z), share_of(member)],
                  wo_zs.at[j], wo_zr.at[j], x * ZS + z_at(j)))

    def share_copy(j):
        return pltpu.make_async_remote_copy(
            src_ref=wo.at[:, share_of(member)], dst_ref=wo.at[:, share_of(member)],
            send_sem=wo_ts.at[j], recv_sem=wo_tr.at[j],
            device_id={"users": team_at + mate(j)}, device_id_type=MESH)

    def share_wo():
        loads[5].wait()
        for j in range(1, ZS):
            come = wo.at[rows_of(z_at(-j)), share_of(member)]
            push(come, come, wo_zr.at[j], wo_zr.at[j], me).wait_recv()
        for j in range(1, team):
            share_copy(j).start()

    for j in range(1, XS):
        come = ids_x.at[x_at(-j)]
        push(come, come, oh_xr.at[j], oh_xr.at[j], me).wait_recv()
    down = lax.broadcasted_iota(jnp.int32, (item_count, group_rows), 0).astype(F32)
    per_tile = XS // tiles
    user_rows = XS * ZS * each
    z_rows = XS * each
    shown = []
    for s in range(XS):
        chosen = jnp.transpose(jnp.where(down == ids_x[s, 0:1, :].astype(F32), 1.0, 0.0))
        shown.append(chosen.reshape(ZS, own, item_count))
    blank = jnp.zeros((ZS, each, item_count), F32)
    for u in range(users):
        wide_rows = []
        for s in range(XS):
            mine = shown[s][:, u * each : (u + 1) * each]
            wide_rows.append(jnp.concatenate(
                [mine if t == s // per_tile else blank for t in range(tiles)], axis=2))
        chooser[u] = jnp.concatenate(wide_rows, axis=1).reshape(
            user_rows, tiles * item_count).astype(BF16)

    def gate_copy(j):
        to = z_at(j)
        return push(gate_out.at[to], gate_in.at[slot], ga_s.at[j], ga_r.at[slot], x * ZS + to)

    def make_gate():
        for j in range(1, XS):
            come = wg.at[group(x_at(-j))]
            push(come, come, wg_xr.at[j], wg_xr.at[j], me).wait_recv()
        gate_items = silu(jnp.dot(normed[...], wg[...], preferred_element_type=F32)).astype(BF16)
        twice = jnp.concatenate([gate_items] * tiles, axis=0)
        for u in range(users):
            gate_out[:, u] = jnp.dot(
                chooser[u], twice, preferred_element_type=F32
            ).astype(BF16).reshape(ZS, z_rows, HEAD_DIM)
        for j in NEAREST[::-1]:
            gate_copy(j).start()
        gate_in[slot] = gate_out[z]

    for load in loads[9:]:
        load.wait()

    pairs = HEADS // 2
    steps = users * pairs

    def place_of(k):
        u, s = lax.div(k, pairs), lax.rem(k, pairs)
        early = lax.div(z, 2) + s + lax.div(s, 2) * (5 - 2 * s)
        late = x + 1 + s
        first = jnp.where(u == 0, 1, 0)
        return u, lax.rem(first * early + (1 - first) * late + 2 * pairs, pairs)

    def part_copy(u, p):
        j = lax.rem(p - x + XS, XS)
        return push(part.at[u, p], part_in.at[u, x], rx_s.at[u * XS + j], rx_r.at[u * XS + j],
                    p * ZS + z)

    def attend(k):
        u, p = place_of(k)
        heads = (2 * p, 2 * p + 1)

        for h in heads:
            @pl.when((k < pairs) & (h != z))
            def _():
                j = lax.rem(z - h + ZS, ZS)
                push(query.at[h], query.at[h], q_r.at[j], q_r.at[j], me).wait_recv()

        nothing = jnp.zeros((item_count, HEAD_DIM), BF16)
        asked = jnp.concatenate([
            jnp.concatenate([query[heads[0]], nothing], axis=1),
            jnp.concatenate([nothing, query[heads[1]]], axis=1)], axis=0)
        columns = pl.ds(pl.multiple_of(p * 2 * HEAD_DIM, 2 * HEAD_DIM), 2 * HEAD_DIM)
        scores = lax.dot_general(
            asked, keys[u, :, columns], (((1,), (1,)), ((), ())), preferred_element_type=F32)
        halved = scores * (0.5 * HEAD_DIM ** (-0.5))
        weight = halved + halved * jnp.tanh(halved)
        kept = jnp.concatenate(
            [(weight * live[u * tiles + t]).astype(BF16) for t in range(tiles)], axis=0)
        sums = jnp.dot(kept, vals[u, :, columns], preferred_element_type=F32)
        both = []
        for t in range(tiles):
            at = t * 2 * item_count
            both.append(jnp.concatenate([
                sums[at : at + item_count, :HEAD_DIM],
                sums[at + item_count : at + 2 * item_count, HEAD_DIM:]], axis=1))
        part[u, p] = jnp.dot(
            chooser[u], jnp.concatenate(both, axis=0).astype(BF16),
            preferred_element_type=F32).astype(BF16)

        @pl.when(p != x)
        def _():
            part_copy(u, p).start()

    def rows_z(at):
        return pl.ds(pl.multiple_of(at * z_rows, z_rows), z_rows)

    def half_copy(u, j):
        to = z_at(j)
        return push(half.at[u, rows_z(to)], half_in.at[u, z], rz_s.at[u * ZS + j], rz_r.at[u * ZS + j],
                    x * ZS + to)

    def reduce_x(u):
        total = part[u, x].astype(F32)
        for j in range(1, XS):
            come = part_in.at[u, x_at(-j)]
            push(come, come, rx_r.at[u * XS + j], rx_r.at[u * XS + j], me).wait_recv()
            total += part_in[u, x_at(-j)].astype(F32)
        half[u] = total.astype(BF16)
        for j in NEAREST[::-1]:
            half_copy(u, j).start()

    def project(u):
        attended = half[u, rows_z(z)].astype(F32)
        for j in NEAREST:
            come = half_in.at[u, z_at(-j)]
            push(come, come, rz_r.at[u * ZS + j], rz_r.at[u * ZS + j], me).wait_recv()
            attended += half_in[u, z_at(-j)].astype(F32)
        squares = attended * attended
        sq[u] = (squares[:, :HEAD_DIM] + squares[:, HEAD_DIM:]).reshape(XS, each, HEAD_DIM)
        gate = jnp.concatenate([gate_in[i, u] for i in range(HEADS // XS)], axis=1).astype(F32)
        width = 2 * HEAD_DIM
        gain = gain_attn[:, pl.ds(pl.multiple_of(x * width, width), width)]
        added = jnp.dot(
            (attended * gain * gate).astype(BF16), wo[...], preferred_element_type=F32
        ).reshape(XS, each, HEADS * HEAD_DIM)
        middle = HEADS * HEAD_DIM // 2
        proj[u] = jnp.concatenate([added[:, :, :middle], added[:, :, middle:]], axis=1).astype(BF16)
        for j in (2, 1, 3):
            to = x_at(j)
            send(push(proj.at[u, to], proj_in.at[u, x], po_s.at[u * XS + j], po_r.at[u * XS + j],
                      to * ZS + z))
            send(push(sq.at[u, to], sq_in.at[u, x], sq_s.at[u * XS + j], sq_r.at[u * XS + j],
                      to * ZS + z))

    def finish(u):
        squares = sq[u, x]
        projected = proj[u, x].astype(F32)
        for j in (1, 3, 2):
            frm = x_at(-j)
            push(proj_in.at[u, frm], proj_in.at[u, frm], po_r.at[u * XS + j], po_r.at[u * XS + j],
                 me).wait_recv()
            projected += proj_in[u, frm].astype(F32)
            push(sq_in.at[u, frm], sq_in.at[u, frm], sq_r.at[u * XS + j], sq_r.at[u * XS + j],
                 me).wait_recv()
            squares += sq_in[u, frm]
        scale = lax.rsqrt(
            jnp.sum(squares, axis=1, keepdims=True) * (1.0 / (HEADS * HEAD_DIM)) + EPSILON)
        projected = jnp.concatenate([projected[:each], projected[each:]], axis=1)
        return tokens[u * each : (u + 1) * each] + projected * scale

    def step(k, carry):
        attend(k)

        @pl.when((k == 1) & (gate_x == x))
        def _():
            make_gate()

        @pl.when(k == steps - 2)
        def _():
            share_wo()
            reduce_x(0)

        return carry

    lax.fori_loop(0, steps, step, 0)
    for u in range(1, users):
        reduce_x(u)
    for i in range(HEADS // XS):
        frm = x * (HEADS // XS) + i

        @pl.when(frm != z)
        def _():
            push(gate_in.at[i], gate_in.at[i], ga_r.at[i], ga_r.at[i], me).wait_recv()
    loads[6].wait()
    for j in range(1, team):
        come = wo.at[:, share_of(lax.rem(member - j + team, team))]
        push(come, come, wo_tr.at[j], wo_tr.at[j], me).wait_recv()
    for u in range(users):
        project(u)
    rows_out = [finish(u) for u in range(users)]
    out[...] = jnp.concatenate(rows_out, axis=0).astype(BF16)

    for copy in sends:
        copy.wait_send()
    for j in range(1, team):
        share_copy(j).wait_send()

    @pl.when(gate_x != x)
    def _():
        wg_copy.wait_send()

    @pl.when(gate_x == x)
    def _():
        for j in range(1, ZS):
            gate_copy(j).wait_send()

    for u in range(users):
        for j in range(1, XS):
            part_copy(u, x_at(j)).wait_send()
        for j in range(1, ZS):
            half_copy(u, j).wait_send()


def on_device(
    cand_items, item_rows, hist_keys, hist_values, block_mask, hist_lengths,
    gain_in, w_query, w_gate, gain_attn, w_out,
):
    row_count, users = cand_items.shape
    item_count, width = item_rows.shape
    events = hist_keys.shape[1]
    rows = w_query.shape[0]
    own = row_count * users
    tiles = block_mask.shape[1]
    user_rows = XS * ZS * row_count
    team = min(TEAM, lax.axis_size("users"))
    dma = pltpu.SemaphoreType.DMA
    anywhere = pl.BlockSpec(memory_space=pl.ANY)
    vmem = pl.BlockSpec(memory_space=pltpu.VMEM)
    ranked = pl.pallas_call(
        kernel,
        out_shape=jax.ShapeDtypeStruct((own, width), BF16),
        in_specs=[anywhere] * 11,
        out_specs=vmem,
        scratch_shapes=[
            pltpu.VMEM((users, row_count), jnp.int32),
            pltpu.SMEM(block_mask.shape, jnp.int32),
            pltpu.SMEM((users,), jnp.int32),
            pltpu.VMEM((1, width), F32),
            pltpu.VMEM((1, width), F32),
            pltpu.VMEM((item_count, width), BF16),
            pltpu.VMEM((users, events, width), BF16),
            pltpu.VMEM((users, events, width), BF16),
            pltpu.VMEM((item_count, width), BF16),
            pltpu.VMEM((ZS, own, item_count), BF16),
            pltpu.VMEM((XS, own, ZS * own), BF16),
            pltpu.VMEM((users, user_rows, tiles * item_count), BF16),
            pltpu.VMEM((users * tiles, 1, events), F32),
            pltpu.VMEM((own, width), F32),
            pltpu.VMEM((XS * ZS * rows, HEAD_DIM), BF16),
            pltpu.VMEM((XS * ZS * rows, HEAD_DIM), BF16),
            pltpu.VMEM((ZS * rows, width), BF16),
            pltpu.VMEM((HEADS, item_count, HEAD_DIM), BF16),
            pltpu.VMEM((ZS, users, user_rows // ZS, HEAD_DIM), BF16),
            pltpu.VMEM((HEADS // XS, users, user_rows // ZS, HEAD_DIM), BF16),
            pltpu.VMEM((users, XS, user_rows, 2 * HEAD_DIM), BF16),
            pltpu.VMEM((users, XS, user_rows, 2 * HEAD_DIM), BF16),
            pltpu.VMEM((users, user_rows, 2 * HEAD_DIM), BF16),
            pltpu.VMEM((users, ZS, user_rows // ZS, 2 * HEAD_DIM), BF16),
            pltpu.VMEM((users, XS, own, width // 2), BF16),
            pltpu.VMEM((users, XS, own, width // 2), BF16),
            pltpu.VMEM((users, XS, row_count, HEAD_DIM), F32),
            pltpu.VMEM((users, XS, row_count, HEAD_DIM), F32),
            dma((9 + 2 * users,)),
            dma((ZS,)), dma((ZS,)), dma((XS,)), dma((XS,)),
            dma((ZS,)), dma((ZS,)), dma((XS,)), dma((XS,)),
            dma((ZS,)), dma((ZS,)), dma((XS,)), dma((XS,)),
            dma((ZS,)), dma((ZS,)), dma((team,)), dma((team,)),
            dma((ZS,)), dma((ZS,)),
            dma((ZS,)), dma((HEADS // XS,)),
            dma((users * XS,)), dma((users * XS,)),
            dma((users * ZS,)), dma((users * ZS,)),
            dma((users * XS,)), dma((users * XS,)),
            dma((users * XS,)), dma((users * XS,)),
        ],
        compiler_params=pltpu.CompilerParams(
            collective_id=0, has_side_effects=True, vmem_limit_bytes=63 * 1024 * 1024),
        cost_estimate=pl.CostEstimate(flops=10**9, bytes_accessed=5 * 10**6, transcendentals=10**6),
        name="ranked",
    )(
        cand_items.T, item_rows, hist_keys, hist_values, block_mask, hist_lengths,
        gain_in.reshape(1, width), w_query, w_gate, gain_attn.reshape(1, width), w_out,
    )
    return ranked.reshape(users, row_count, width).transpose(1, 0, 2)


def solution(mesh):
    in_specs = (
        P(("users", "seq"), None),
        P("users", None),
        P("users", "seq", None),
        P("users", "seq", None),
        P("users", None, "seq"),
        P("users"),
        P(),
        P("seq", None),
        P("seq", None),
        P(),
        P("seq", None),
    )
    out_specs = P(("users", "seq"), None, None)
    return jax.shard_map(
        on_device, mesh=mesh, in_specs=in_specs, out_specs=out_specs, check_vma=False
    )
```

```python
import jax
import jax.numpy as jnp
from jax import lax
from jax.experimental import pallas as pl
from jax.experimental.pallas import tpu as pltpu
from jax.sharding import PartitionSpec as P

HEADS = 8
HEAD_DIM = 128
BLOCK = 128
EPSILON = 1e-06
XS, ZS = 4, 8
NEAREST = (7, 1, 6, 2, 5, 3, 4)
TEAM = 4
MESH = pl.DeviceIdType.MESH
BF16, F32 = jnp.bfloat16, jnp.float32


def silu(v):
    return v / (1.0 + jnp.exp(-v))


def push(src, dst, send_sem, recv_sem, seq):
    return pltpu.make_async_remote_copy(
        src_ref=src, dst_ref=dst, send_sem=send_sem, recv_sem=recv_sem,
        device_id={"seq": seq}, device_id_type=MESH)


def kernel(
    cand_hbm, items_hbm, keys_hbm, vals_hbm, mask_hbm, lens_hbm, gain_in_hbm, wq_hbm, wg_hbm,
    gain_attn_hbm, wo_hbm,
    out,
    cand, mask, lens, gain_in, gain_attn, items, keys, vals, normed, picks, ids_x, chooser, live,
    tokens, wq, wg, wo, query, gate_out, gate_in, part, relay, part_in, half, half_in, proj, proj_in, sq, sq_in,
    load_sem, wq_zs, wq_zr, wq_xs, wq_xr, wg_zs, wg_zr, wg_xs, wg_xr, oh_zs, oh_zr, oh_xs, oh_xr,
    wo_zs, wo_zr, wo_ts, wo_tr, q_s, q_r, ga_s, ga_r, rl_s, rl_r, rx_s, rx_r, rz_s, rz_r, po_s, po_r, sq_s, sq_r,
):
    me = lax.axis_index("seq")
    x, z = lax.div(me, ZS), lax.rem(me, ZS)
    team = min(TEAM, lax.axis_size("users"))
    member = lax.rem(lax.axis_index("users"), team)
    team_at = lax.axis_index("users") - member
    rows = wq_hbm.shape[0]
    own = picks.shape[1]
    tiles = mask.shape[1]
    users, events = keys_hbm.shape[0], keys_hbm.shape[1]
    item_count = items_hbm.shape[0]

    def z_at(step):
        return lax.rem(z + step + ZS, ZS)

    def x_at(step):
        return lax.rem(x + step + XS, XS)

    def lanes(index):
        return pl.ds(pl.multiple_of(index * HEAD_DIM, HEAD_DIM), HEAD_DIM)

    def rows_of(seq):
        return pl.ds(pl.multiple_of(seq * rows, rows), rows)

    share = wo_hbm.shape[1] // team

    def share_of(at):
        return pl.ds(pl.multiple_of(at * share, share), share)

    def mate(step):
        return lax.rem(member + step, team)

    barrier = pltpu.get_barrier_semaphore()
    for j in range(1, ZS):
        pl.semaphore_signal(barrier, inc=1, device_id={"seq": x * ZS + z_at(j)}, device_id_type=MESH)
    for j in range(1, XS):
        pl.semaphore_signal(barrier, inc=1, device_id={"seq": x_at(j) * ZS + z}, device_id_type=MESH)

    for j in range(1, team):
        pl.semaphore_signal(barrier, inc=1, device_id={"users": team_at + mate(j)}, device_id_type=MESH)

    loads = [
        pltpu.make_async_copy(cand_hbm, cand, load_sem.at[0]),
        pltpu.make_async_copy(items_hbm, items, load_sem.at[1]),
        pltpu.make_async_copy(gain_in_hbm, gain_in, load_sem.at[2]),
        pltpu.make_async_copy(wq_hbm.at[:, lanes(z)], wq.at[rows_of(me)], load_sem.at[3]),
        pltpu.make_async_copy(wg_hbm.at[:, lanes(z)], wg.at[rows_of(me)], load_sem.at[4]),
        pltpu.make_async_copy(
            wo_hbm.at[:, share_of(member)], wo.at[rows_of(z), share_of(member)], load_sem.at[5]),
        pltpu.make_async_copy(gain_attn_hbm, gain_attn, load_sem.at[6]),
        pltpu.make_async_copy(mask_hbm, mask, load_sem.at[7]),
        pltpu.make_async_copy(lens_hbm, lens, load_sem.at[8]),
    ]
    for u in range(users):
        loads.append(pltpu.make_async_copy(keys_hbm.at[u], keys.at[u], load_sem.at[9 + 2 * u]))
        loads.append(pltpu.make_async_copy(vals_hbm.at[u], vals.at[u], load_sem.at[10 + 2 * u]))
    for load in loads[:4]:
        load.start()

    pl.semaphore_wait(barrier, XS + ZS + team - 3)

    sends = []

    def send(copy):
        copy.start()
        sends.append(copy)

    for j in range(1, ZS):
        to = z_at(j)
        send(push(wq_hbm.at[:, lanes(to)], wq.at[rows_of(me)], wq_zs.at[j], wq_zr.at[j], x * ZS + to))
    for load in loads[4:]:
        load.start()

    loads[0].wait()
    each = own // users
    row = lax.broadcasted_iota(jnp.int32, (own, each), 0)
    column = lax.broadcasted_iota(jnp.int32, (own, each), 1)
    ids = jnp.zeros((own, 1), F32)
    for u in range(users):
        here = row == column + u * each
        ids += jnp.sum(
            jnp.where(here, cand[u : u + 1, :].astype(F32), 0.0), axis=1, keepdims=True)
    item = lax.broadcasted_iota(jnp.int32, (own, item_count), 1).astype(F32)
    own_pick = jnp.where(item == ids, 1.0, 0.0).astype(BF16)
    picks[z] = own_pick

    for j in range(1, ZS):
        send(push(picks.at[z], picks.at[z], oh_zs.at[j], oh_zr.at[j], x * ZS + z_at(j)))

    loads[1].wait()
    loads[2].wait()
    wide = items[...].astype(F32)
    normed[...] = (
        wide * lax.rsqrt(jnp.mean(wide * wide, axis=-1, keepdims=True) + EPSILON) * gain_in[...]
    ).astype(BF16)

    def group(at):
        return pl.ds(pl.multiple_of(at * (ZS * rows), ZS * rows), ZS * rows)

    loads[3].wait()
    for j in range(1, ZS):
        come = wq.at[rows_of(x * ZS + z_at(-j))]
        push(come, come, wq_zr.at[j], wq_zr.at[j], me).wait_recv()
    for j in range(1, XS):
        send(push(wq.at[group(x)], wq.at[group(x)], wq_xs.at[j], wq_xr.at[j], x_at(j) * ZS + z))

    for j in range(1, ZS):
        to = z_at(j)
        send(push(wg_hbm.at[:, lanes(to)], wg.at[rows_of(me)], wg_zs.at[j], wg_zr.at[j], x * ZS + to))

    for j in range(1, ZS):
        come = picks.at[z_at(-j)]
        push(come, come, oh_zr.at[j], oh_zr.at[j], me).wait_recv()
    group_rows = ZS * own
    picked = picks[...].reshape(group_rows, item_count)
    number = lax.broadcasted_iota(jnp.int32, (own, item_count), 1).astype(F32).astype(BF16)
    ids_x[x] = lax.dot_general(
        number, picked, (((1,), (1,)), ((), ())), preferred_element_type=F32).astype(BF16)
    for j in range(1, XS):
        send(push(ids_x.at[x], ids_x.at[x], oh_xs.at[j], oh_xr.at[j], x_at(j) * ZS + z))

    tokens[...] = jnp.dot(own_pick, items[...], preferred_element_type=F32)
    loads[7].wait()
    loads[8].wait()
    for u in range(users):
        length = lens[u] - me * events
        for t in range(tiles):
            for b in range(events // BLOCK):
                place = b * BLOCK + lax.broadcasted_iota(jnp.int32, (1, BLOCK), 1)
                opened = jnp.full((1, BLOCK), mask[u, t, b], jnp.int32)
                live[u * tiles + t, :, pl.ds(b * BLOCK, BLOCK)] = jnp.where(
                    (opened == 1) & (place < length), 1.0, 0.0)

    for j in range(1, XS):
        come = wq.at[group(x_at(-j))]
        push(come, come, wq_xr.at[j], wq_xr.at[j], me).wait_recv()
    query[z] = silu(jnp.dot(normed[...], wq[...], preferred_element_type=F32)).astype(BF16)
    for j in NEAREST:
        send(push(query.at[z], query.at[z], q_s.at[j], q_r.at[j], x * ZS + z_at(j)))

    gate_x = lax.div(z, HEADS // XS)
    gate_step = lax.rem(gate_x - x + XS, XS)
    wg_copy = push(wg.at[group(x)], wg.at[group(x)], wg_xs.at[gate_step], wg_xr.at[gate_step],
                   gate_x * ZS + z)
    slot = lax.rem(z, HEADS // XS)
    def share_part(j):
        return push(wo_hbm.at[:, share_of(member)], wo.at[rows_of(z), share_of(member)],
                    wo_zs.at[j], wo_zr.at[j], x * ZS + z_at(j))

    def pass_weights():
        loads[4].wait()
        for j in range(1, ZS):
            come = wg.at[rows_of(x * ZS + z_at(-j))]
            push(come, come, wg_zr.at[j], wg_zr.at[j], me).wait_recv()

        @pl.when(gate_x != x)
        def _():
            wg_copy.start()

        for j in range(1, ZS):
            share_part(j).start()

    def share_copy(j):
        return pltpu.make_async_remote_copy(
            src_ref=wo.at[:, share_of(member)], dst_ref=wo.at[:, share_of(member)],
            send_sem=wo_ts.at[j], recv_sem=wo_tr.at[j],
            device_id={"users": team_at + mate(j)}, device_id_type=MESH)

    def share_wo():
        loads[5].wait()
        for j in range(1, ZS):
            come = wo.at[rows_of(z_at(-j)), share_of(member)]
            push(come, come, wo_zr.at[j], wo_zr.at[j], me).wait_recv()
        for j in range(1, team):
            share_copy(j).start()

    for j in range(1, XS):
        come = ids_x.at[x_at(-j)]
        push(come, come, oh_xr.at[j], oh_xr.at[j], me).wait_recv()
    down = lax.broadcasted_iota(jnp.int32, (item_count, group_rows), 0).astype(F32)
    per_tile = XS // tiles
    user_rows = XS * ZS * each
    z_rows = XS * each
    shown = []
    for s in range(XS):
        chosen = jnp.transpose(jnp.where(down == ids_x[s, 0:1, :].astype(F32), 1.0, 0.0))
        shown.append(chosen.reshape(ZS, own, item_count))
    blank = jnp.zeros((ZS, each, item_count), F32)
    for u in range(users):
        wide_rows = []
        for s in range(XS):
            mine = shown[s][:, u * each : (u + 1) * each]
            wide_rows.append(jnp.concatenate(
                [mine if t == s // per_tile else blank for t in range(tiles)], axis=2))
        chooser[u] = jnp.concatenate(wide_rows, axis=1).reshape(
            user_rows, tiles * item_count).astype(BF16)

    def gate_copy(j):
        to = z_at(j)
        return push(gate_out.at[to], gate_in.at[slot], ga_s.at[j], ga_r.at[slot], x * ZS + to)

    def make_gate():
        for j in range(1, XS):
            come = wg.at[group(x_at(-j))]
            push(come, come, wg_xr.at[j], wg_xr.at[j], me).wait_recv()
        gate_items = silu(jnp.dot(normed[...], wg[...], preferred_element_type=F32)).astype(BF16)
        twice = jnp.concatenate([gate_items] * tiles, axis=0)
        for u in range(users):
            gate_out[:, u] = jnp.dot(
                chooser[u], twice, preferred_element_type=F32
            ).astype(BF16).reshape(ZS, z_rows, HEAD_DIM)
        for j in NEAREST[::-1]:
            gate_copy(j).start()
        gate_in[slot] = gate_out[z]

    for load in loads[9:]:
        load.wait()

    pairs = HEADS // 2
    steps = users * pairs
    lag = 2

    def place_of(k):
        u, s = lax.div(k, pairs), lax.rem(k, pairs)
        early = lax.div(z, 2) + s + lax.div(s, 2) * (5 - 2 * s)
        late = x + 1 + s
        first = jnp.where(u == 0, 1, 0)
        return u, lax.rem(first * early + (1 - first) * late + 2 * pairs, pairs)

    def part_copy(u, p):
        j = lax.rem(p - x + XS, XS)
        return push(part.at[u, p], part_in.at[u, x], rx_s.at[u * XS + j], rx_r.at[u * XS + j],
                    p * ZS + z)

    def attend(k):
        u, p = place_of(k)
        heads = (2 * p, 2 * p + 1)

        for h in heads:
            @pl.when((k < pairs) & (h != z))
            def _():
                j = lax.rem(z - h + ZS, ZS)
                push(query.at[h], query.at[h], q_r.at[j], q_r.at[j], me).wait_recv()

        nothing = jnp.zeros((item_count, HEAD_DIM), BF16)
        asked = jnp.concatenate([
            jnp.concatenate([query[heads[0]], nothing], axis=1),
            jnp.concatenate([nothing, query[heads[1]]], axis=1)], axis=0)
        columns = pl.ds(pl.multiple_of(p * 2 * HEAD_DIM, 2 * HEAD_DIM), 2 * HEAD_DIM)
        scores = lax.dot_general(
            asked, keys[u, :, columns], (((1,), (1,)), ((), ())), preferred_element_type=F32)
        halved = scores * (0.5 * HEAD_DIM ** (-0.5))
        weight = halved + halved * jnp.tanh(halved)
        kept = jnp.concatenate(
            [(weight * live[u * tiles + t]).astype(BF16) for t in range(tiles)], axis=0)
        sums = jnp.dot(kept, vals[u, :, columns], preferred_element_type=F32)
        both = []
        for t in range(tiles):
            at = t * 2 * item_count
            both.append(jnp.concatenate([
                sums[at : at + item_count, :HEAD_DIM],
                sums[at + item_count : at + 2 * item_count, HEAD_DIM:]], axis=1))
        part[u, p] = jnp.dot(
            chooser[u], jnp.concatenate(both, axis=0).astype(BF16),
            preferred_element_type=F32).astype(BF16)

        @pl.when((u > 0) & (p != x))
        def _():
            part_copy(u, p).start()

        role = lax.rem(x - p + XS, XS)

        @pl.when((u == 0) & (role == 2))
        def _():
            relay_copy(0).start()
            relay_copy(1).start()

        @pl.when((u == 0) & (role == 1))
        def _():
            near_copy(0, 1).start()

        @pl.when((u == 0) & (role == 3))
        def _():
            near_copy(1, 0).start()

    sides = (x_at(-1), x_at(1))
    middle_row = chooser.shape[1] // 2
    halves = (pl.ds(0, middle_row), pl.ds(middle_row, middle_row))

    def relay_copy(i):
        return push(part.at[0, x_at(2), halves[i]], relay.at[i], rl_s.at[i], rl_r.at[i],
                    sides[i] * ZS + z)

    def near_copy(side, i):
        return push(part.at[0, sides[side], halves[i]], part_in.at[0, side, halves[i]],
                    rx_s.at[side * 2 + i], rx_r.at[side * 2 + i], sides[side] * ZS + z)

    def pass_on(k):
        u, p = place_of(k)
        for i in range(2):
            @pl.when(p == sides[i])
            def _():
                relay_copy(i).wait_recv()
                part[0, p, halves[i]] = (
                    part[0, p, halves[i]].astype(F32) + relay[i].astype(F32)).astype(BF16)
                near_copy(i, i).start()

    def rows_z(at):
        return pl.ds(pl.multiple_of(at * z_rows, z_rows), z_rows)

    def half_copy(u, j):
        to = z_at(j)
        return push(half.at[u, rows_z(to)], half_in.at[u, z], rz_s.at[u * ZS + j], rz_r.at[u * ZS + j],
                    x * ZS + to)

    def reduce_x(u):
        total = part[u, x].astype(F32)
        if u == 0:
            for side in range(2):
                for i in range(2):
                    near_copy(side, i).wait_recv()
                total += part_in[0, side].astype(F32)
        else:
            for j in range(1, XS):
                come = part_in.at[u, x_at(-j)]
                push(come, come, rx_r.at[u * XS + j], rx_r.at[u * XS + j], me).wait_recv()
                total += part_in[u, x_at(-j)].astype(F32)
        half[u] = total.astype(BF16)
        for j in NEAREST[::-1]:
            half_copy(u, j).start()

    def project(u):
        attended = half[u, rows_z(z)].astype(F32)
        for j in NEAREST:
            come = half_in.at[u, z_at(-j)]
            push(come, come, rz_r.at[u * ZS + j], rz_r.at[u * ZS + j], me).wait_recv()
            attended += half_in[u, z_at(-j)].astype(F32)
        squares = attended * attended
        sq[u] = (squares[:, :HEAD_DIM] + squares[:, HEAD_DIM:]).reshape(XS, each, HEAD_DIM)
        gate = jnp.concatenate([gate_in[i, u] for i in range(HEADS // XS)], axis=1).astype(F32)
        width = 2 * HEAD_DIM
        gain = gain_attn[:, pl.ds(pl.multiple_of(x * width, width), width)]
        added = jnp.dot(
            (attended * gain * gate).astype(BF16), wo[...], preferred_element_type=F32
        ).reshape(XS, each, HEADS * HEAD_DIM)
        middle = HEADS * HEAD_DIM // 2
        proj[u] = jnp.concatenate([added[:, :, :middle], added[:, :, middle:]], axis=1).astype(BF16)
        for j in (2, 1, 3):
            to = x_at(j)
            send(push(proj.at[u, to], proj_in.at[u, x], po_s.at[u * XS + j], po_r.at[u * XS + j],
                      to * ZS + z))
            send(push(sq.at[u, to], sq_in.at[u, x], sq_s.at[u * XS + j], sq_r.at[u * XS + j],
                      to * ZS + z))

    def finish(u):
        squares = sq[u, x]
        projected = proj[u, x].astype(F32)
        for j in (1, 3, 2):
            frm = x_at(-j)
            push(proj_in.at[u, frm], proj_in.at[u, frm], po_r.at[u * XS + j], po_r.at[u * XS + j],
                 me).wait_recv()
            projected += proj_in[u, frm].astype(F32)
            push(sq_in.at[u, frm], sq_in.at[u, frm], sq_r.at[u * XS + j], sq_r.at[u * XS + j],
                 me).wait_recv()
            squares += sq_in[u, frm]
        scale = lax.rsqrt(
            jnp.sum(squares, axis=1, keepdims=True) * (1.0 / (HEADS * HEAD_DIM)) + EPSILON)
        projected = jnp.concatenate([projected[:each], projected[each:]], axis=1)
        return tokens[u * each : (u + 1) * each] + projected * scale

    def step(k, carry):
        attend(k)

        @pl.when(k == 0)
        def _():
            pass_weights()

        @pl.when((k == 2) & (gate_x == x))
        def _():
            make_gate()

        @pl.when((k >= lag) & (k < pairs + lag))
        def _():
            pass_on(k - lag)

        @pl.when(k == steps - 2)
        def _():
            share_wo()
            reduce_x(0)

        return carry

    lax.fori_loop(0, steps, step, 0)
    for u in range(1, users):
        reduce_x(u)
    for i in range(HEADS // XS):
        frm = x * (HEADS // XS) + i

        @pl.when(frm != z)
        def _():
            push(gate_in.at[i], gate_in.at[i], ga_r.at[i], ga_r.at[i], me).wait_recv()
    loads[6].wait()
    for j in range(1, team):
        come = wo.at[:, share_of(lax.rem(member - j + team, team))]
        push(come, come, wo_tr.at[j], wo_tr.at[j], me).wait_recv()
    rows_out = []
    for u in range(users):
        project(u)
        rows_out.append(finish(u))
    out[...] = jnp.concatenate(rows_out, axis=0).astype(BF16)

    for copy in sends:
        copy.wait_send()
    for j in range(1, team):
        share_copy(j).wait_send()

    @pl.when(gate_x != x)
    def _():
        wg_copy.wait_send()

    @pl.when(gate_x == x)
    def _():
        for j in range(1, ZS):
            gate_copy(j).wait_send()

    for j in range(1, ZS):
        share_part(j).wait_send()
    for i in range(2):
        relay_copy(i).wait_send()
        for side in range(2):
            near_copy(side, i).wait_send()
    for u in range(users):
        for j in range(1, XS if u > 0 else 1):
            part_copy(u, x_at(j)).wait_send()
        for j in range(1, ZS):
            half_copy(u, j).wait_send()


def on_device(
    cand_items, item_rows, hist_keys, hist_values, block_mask, hist_lengths,
    gain_in, w_query, w_gate, gain_attn, w_out,
):
    row_count, users = cand_items.shape
    item_count, width = item_rows.shape
    events = hist_keys.shape[1]
    rows = w_query.shape[0]
    own = row_count * users
    tiles = block_mask.shape[1]
    user_rows = XS * ZS * row_count
    team = min(TEAM, lax.axis_size("users"))
    dma = pltpu.SemaphoreType.DMA
    anywhere = pl.BlockSpec(memory_space=pl.ANY)
    vmem = pl.BlockSpec(memory_space=pltpu.VMEM)
    ranked = pl.pallas_call(
        kernel,
        out_shape=jax.ShapeDtypeStruct((own, width), BF16),
        in_specs=[anywhere] * 11,
        out_specs=vmem,
        scratch_shapes=[
            pltpu.VMEM((users, row_count), jnp.int32),
            pltpu.SMEM(block_mask.shape, jnp.int32),
            pltpu.SMEM((users,), jnp.int32),
            pltpu.VMEM((1, width), F32),
            pltpu.VMEM((1, width), F32),
            pltpu.VMEM((item_count, width), BF16),
            pltpu.VMEM((users, events, width), BF16),
            pltpu.VMEM((users, events, width), BF16),
            pltpu.VMEM((item_count, width), BF16),
            pltpu.VMEM((ZS, own, item_count), BF16),
            pltpu.VMEM((XS, own, ZS * own), BF16),
            pltpu.VMEM((users, user_rows, tiles * item_count), BF16),
            pltpu.VMEM((users * tiles, 1, events), F32),
            pltpu.VMEM((own, width), F32),
            pltpu.VMEM((XS * ZS * rows, HEAD_DIM), BF16),
            pltpu.VMEM((XS * ZS * rows, HEAD_DIM), BF16),
            pltpu.VMEM((ZS * rows, width), BF16),
            pltpu.VMEM((HEADS, item_count, HEAD_DIM), BF16),
            pltpu.VMEM((ZS, users, user_rows // ZS, HEAD_DIM), BF16),
            pltpu.VMEM((HEADS // XS, users, user_rows // ZS, HEAD_DIM), BF16),
            pltpu.VMEM((users, XS, user_rows, 2 * HEAD_DIM), BF16),
            pltpu.VMEM((2, user_rows // 2, 2 * HEAD_DIM), BF16),
            pltpu.VMEM((users, XS, user_rows, 2 * HEAD_DIM), BF16),
            pltpu.VMEM((users, user_rows, 2 * HEAD_DIM), BF16),
            pltpu.VMEM((users, ZS, user_rows // ZS, 2 * HEAD_DIM), BF16),
            pltpu.VMEM((users, XS, own, width // 2), BF16),
            pltpu.VMEM((users, XS, own, width // 2), BF16),
            pltpu.VMEM((users, XS, row_count, HEAD_DIM), F32),
            pltpu.VMEM((users, XS, row_count, HEAD_DIM), F32),
            dma((9 + 2 * users,)),
            dma((ZS,)), dma((ZS,)), dma((XS,)), dma((XS,)),
            dma((ZS,)), dma((ZS,)), dma((XS,)), dma((XS,)),
            dma((ZS,)), dma((ZS,)), dma((XS,)), dma((XS,)),
            dma((ZS,)), dma((ZS,)), dma((team,)), dma((team,)),
            dma((ZS,)), dma((ZS,)),
            dma((ZS,)), dma((HEADS // XS,)),
            dma((2,)), dma((2,)),
            dma((users * XS,)), dma((users * XS,)),
            dma((users * ZS,)), dma((users * ZS,)),
            dma((users * XS,)), dma((users * XS,)),
            dma((users * XS,)), dma((users * XS,)),
        ],
        compiler_params=pltpu.CompilerParams(
            collective_id=0, has_side_effects=True, vmem_limit_bytes=63 * 1024 * 1024),
        cost_estimate=pl.CostEstimate(flops=10**9, bytes_accessed=5 * 10**6, transcendentals=10**6),
        name="ranked",
    )(
        cand_items.T, item_rows, hist_keys, hist_values, block_mask, hist_lengths,
        gain_in.reshape(1, width), w_query, w_gate, gain_attn.reshape(1, width), w_out,
    )
    return ranked.reshape(users, row_count, width).transpose(1, 0, 2)


def solution(mesh):
    in_specs = (
        P(("users", "seq"), None),
        P("users", None),
        P("users", "seq", None),
        P("users", "seq", None),
        P("users", None, "seq"),
        P("users"),
        P(),
        P("seq", None),
        P("seq", None),
        P(),
        P("seq", None),
    )
    out_specs = P(("users", "seq"), None, None)
    return jax.shard_map(
        on_device, mesh=mesh, in_specs=in_specs, out_specs=out_specs, check_vma=False
    )
```

```python
import jax
import jax.numpy as jnp
from jax import lax
from jax.experimental import pallas as pl
from jax.experimental.pallas import tpu as pltpu
from jax.sharding import PartitionSpec as P

HEADS = 8
HEAD_DIM = 128
BLOCK = 128
EPSILON = 1e-06
XS, ZS = 4, 8
NEAREST = (7, 1, 6, 2, 5, 3, 4)
TEAM = 4
MESH = pl.DeviceIdType.MESH
BF16, F32 = jnp.bfloat16, jnp.float32


def silu(v):
    return v / (1.0 + jnp.exp(-v))


def push(src, dst, send_sem, recv_sem, seq):
    return pltpu.make_async_remote_copy(
        src_ref=src, dst_ref=dst, send_sem=send_sem, recv_sem=recv_sem,
        device_id={"seq": seq}, device_id_type=MESH)


def kernel(
    cand_hbm, items_hbm, keys_hbm, vals_hbm, mask_hbm, lens_hbm, gain_in_hbm, wq_hbm, wg_hbm,
    gain_attn_hbm, wo_hbm,
    out,
    cand, mask, lens, gain_in, gain_attn, items, keys, vals, normed, picks, ids_x, chooser, live,
    tokens, wq, wg, wo, query, gate_out, gate_in, part, part_in, half, half_in, proj, proj_in, sq, sq_in,
    load_sem, wq_zs, wq_zr, wq_xs, wq_xr, wg_zs, wg_zr, wg_xs, wg_xr, oh_zs, oh_zr, oh_xs, oh_xr,
    wo_zs, wo_zr, wo_ts, wo_tr, q_s, q_r, ga_s, ga_r, rx_s, rx_r, rz_s, rz_r, po_s, po_r, sq_s, sq_r,
):
    me = lax.axis_index("seq")
    x, z = lax.div(me, ZS), lax.rem(me, ZS)
    team = min(TEAM, lax.axis_size("users"))
    member = lax.rem(lax.axis_index("users"), team)
    team_at = lax.axis_index("users") - member
    rows = wq_hbm.shape[0]
    own = picks.shape[1]
    tiles = mask.shape[1]
    users, events = keys_hbm.shape[0], keys_hbm.shape[1]
    item_count = items_hbm.shape[0]

    def z_at(step):
        return lax.rem(z + step + ZS, ZS)

    def x_at(step):
        return lax.rem(x + step + XS, XS)

    def lanes(index):
        return pl.ds(pl.multiple_of(index * HEAD_DIM, HEAD_DIM), HEAD_DIM)

    def rows_of(seq):
        return pl.ds(pl.multiple_of(seq * rows, rows), rows)

    share = wo_hbm.shape[1] // team

    def share_of(at):
        return pl.ds(pl.multiple_of(at * share, share), share)

    def mate(step):
        return lax.rem(member + step, team)

    barrier = pltpu.get_barrier_semaphore()
    for j in range(1, ZS):
        pl.semaphore_signal(barrier, inc=1, device_id={"seq": x * ZS + z_at(j)}, device_id_type=MESH)
    for j in range(1, XS):
        pl.semaphore_signal(barrier, inc=1, device_id={"seq": x_at(j) * ZS + z}, device_id_type=MESH)

    for j in range(1, team):
        pl.semaphore_signal(barrier, inc=1, device_id={"users": team_at + mate(j)}, device_id_type=MESH)

    loads = [
        pltpu.make_async_copy(cand_hbm, cand, load_sem.at[0]),
        pltpu.make_async_copy(items_hbm, items, load_sem.at[1]),
        pltpu.make_async_copy(gain_in_hbm, gain_in, load_sem.at[2]),
        pltpu.make_async_copy(wq_hbm.at[:, lanes(z)], wq.at[rows_of(me)], load_sem.at[3]),
        pltpu.make_async_copy(wg_hbm.at[:, lanes(z)], wg.at[rows_of(me)], load_sem.at[4]),
        pltpu.make_async_copy(
            wo_hbm.at[:, share_of(member)], wo.at[rows_of(z), share_of(member)], load_sem.at[5]),
        pltpu.make_async_copy(gain_attn_hbm, gain_attn, load_sem.at[6]),
        pltpu.make_async_copy(mask_hbm, mask, load_sem.at[7]),
        pltpu.make_async_copy(lens_hbm, lens, load_sem.at[8]),
    ]
    for u in range(users):
        loads.append(pltpu.make_async_copy(keys_hbm.at[u], keys.at[u], load_sem.at[9 + 2 * u]))
        loads.append(pltpu.make_async_copy(vals_hbm.at[u], vals.at[u], load_sem.at[10 + 2 * u]))
    for load in loads[:4]:
        load.start()

    pl.semaphore_wait(barrier, XS + ZS + team - 3)

    sends = []

    def send(copy):
        copy.start()
        sends.append(copy)

    for j in range(1, ZS):
        to = z_at(j)
        send(push(wq_hbm.at[:, lanes(to)], wq.at[rows_of(me)], wq_zs.at[j], wq_zr.at[j], x * ZS + to))
    for load in loads[4:]:
        load.start()

    loads[0].wait()
    each = own // users
    row = lax.broadcasted_iota(jnp.int32, (own, each), 0)
    column = lax.broadcasted_iota(jnp.int32, (own, each), 1)
    ids = jnp.zeros((own, 1), F32)
    for u in range(users):
        here = row == column + u * each
        ids += jnp.sum(
            jnp.where(here, cand[u : u + 1, :].astype(F32), 0.0), axis=1, keepdims=True)
    item = lax.broadcasted_iota(jnp.int32, (own, item_count), 1).astype(F32)
    own_pick = jnp.where(item == ids, 1.0, 0.0).astype(BF16)
    picks[z] = own_pick

    for j in range(1, ZS):
        send(push(picks.at[z], picks.at[z], oh_zs.at[j], oh_zr.at[j], x * ZS + z_at(j)))

    loads[1].wait()
    loads[2].wait()
    wide = items[...].astype(F32)
    normed[...] = (
        wide * lax.rsqrt(jnp.mean(wide * wide, axis=-1, keepdims=True) + EPSILON) * gain_in[...]
    ).astype(BF16)

    def group(at):
        return pl.ds(pl.multiple_of(at * (ZS * rows), ZS * rows), ZS * rows)

    loads[3].wait()
    for j in range(1, ZS):
        come = wq.at[rows_of(x * ZS + z_at(-j))]
        push(come, come, wq_zr.at[j], wq_zr.at[j], me).wait_recv()
    for j in range(1, XS):
        send(push(wq.at[group(x)], wq.at[group(x)], wq_xs.at[j], wq_xr.at[j], x_at(j) * ZS + z))

    for j in range(1, ZS):
        to = z_at(j)
        send(push(wg_hbm.at[:, lanes(to)], wg.at[rows_of(me)], wg_zs.at[j], wg_zr.at[j], x * ZS + to))

    for j in range(1, ZS):
        send(push(wo_hbm.at[:, share_of(member)], wo.at[rows_of(z), share_of(member)],
                  wo_zs.at[j], wo_zr.at[j], x * ZS + z_at(j)))

    for j in range(1, ZS):
        come = picks.at[z_at(-j)]
        push(come, come, oh_zr.at[j], oh_zr.at[j], me).wait_recv()
    group_rows = ZS * own
    picked = picks[...].reshape(group_rows, item_count)
    number = lax.broadcasted_iota(jnp.int32, (own, item_count), 1).astype(F32).astype(BF16)
    ids_x[x] = lax.dot_general(
        number, picked, (((1,), (1,)), ((), ())), preferred_element_type=F32).astype(BF16)
    for j in range(1, XS):
        send(push(ids_x.at[x], ids_x.at[x], oh_xs.at[j], oh_xr.at[j], x_at(j) * ZS + z))

    tokens[...] = jnp.dot(own_pick, items[...], preferred_element_type=F32)
    loads[7].wait()
    loads[8].wait()
    for u in range(users):
        length = lens[u] - me * events
        for t in range(tiles):
            for b in range(events // BLOCK):
                place = b * BLOCK + lax.broadcasted_iota(jnp.int32, (1, BLOCK), 1)
                opened = jnp.full((1, BLOCK), mask[u, t, b], jnp.int32)
                live[u * tiles + t, :, pl.ds(b * BLOCK, BLOCK)] = jnp.where(
                    (opened == 1) & (place < length), 1.0, 0.0)

    for j in range(1, XS):
        come = wq.at[group(x_at(-j))]
        push(come, come, wq_xr.at[j], wq_xr.at[j], me).wait_recv()
    query[z] = silu(jnp.dot(normed[...], wq[...], preferred_element_type=F32)).astype(BF16)
    for j in NEAREST:
        send(push(query.at[z], query.at[z], q_s.at[j], q_r.at[j], x * ZS + z_at(j)))

    gate_x = lax.div(z, HEADS // XS)
    gate_step = lax.rem(gate_x - x + XS, XS)
    wg_copy = push(wg.at[group(x)], wg.at[group(x)], wg_xs.at[gate_step], wg_xr.at[gate_step],
                   gate_x * ZS + z)
    slot = lax.rem(z, HEADS // XS)
    loads[4].wait()
    for j in range(1, ZS):
        come = wg.at[rows_of(x * ZS + z_at(-j))]
        push(come, come, wg_zr.at[j], wg_zr.at[j], me).wait_recv()

    @pl.when(gate_x != x)
    def _():
        wg_copy.start()

    def share_copy(j):
        return pltpu.make_async_remote_copy(
            src_ref=wo.at[:, share_of(member)], dst_ref=wo.at[:, share_of(member)],
            send_sem=wo_ts.at[j], recv_sem=wo_tr.at[j],
            device_id={"users": team_at + mate(j)}, device_id_type=MESH)

    def share_wo():
        loads[5].wait()
        for j in range(1, ZS):
            come = wo.at[rows_of(z_at(-j)), share_of(member)]
            push(come, come, wo_zr.at[j], wo_zr.at[j], me).wait_recv()
        for j in range(1, team):
            share_copy(j).start()

    for j in range(1, XS):
        come = ids_x.at[x_at(-j)]
        push(come, come, oh_xr.at[j], oh_xr.at[j], me).wait_recv()
    down = lax.broadcasted_iota(jnp.int32, (item_count, group_rows), 0).astype(F32)
    per_tile = XS // tiles
    user_rows = XS * ZS * each
    z_rows = XS * each
    shown = []
    for s in range(XS):
        chosen = jnp.transpose(jnp.where(down == ids_x[s, 0:1, :].astype(F32), 1.0, 0.0))
        shown.append(chosen.reshape(ZS, own, item_count))
    blank = jnp.zeros((ZS, each, item_count), F32)
    for u in range(users):
        wide_rows = []
        for s in range(XS):
            mine = shown[s][:, u * each : (u + 1) * each]
            wide_rows.append(jnp.concatenate(
                [mine if t == s // per_tile else blank for t in range(tiles)], axis=2))
        chooser[u] = jnp.concatenate(wide_rows, axis=1).reshape(
            user_rows, tiles * item_count).astype(BF16)

    def gate_copy(j):
        to = z_at(j)
        return push(gate_out.at[to], gate_in.at[slot], ga_s.at[j], ga_r.at[slot], x * ZS + to)

    def make_gate():
        for j in range(1, XS):
            come = wg.at[group(x_at(-j))]
            push(come, come, wg_xr.at[j], wg_xr.at[j], me).wait_recv()
        gate_items = silu(jnp.dot(normed[...], wg[...], preferred_element_type=F32)).astype(BF16)
        twice = jnp.concatenate([gate_items] * tiles, axis=0)
        for u in range(users):
            gate_out[:, u] = jnp.dot(
                chooser[u], twice, preferred_element_type=F32
            ).astype(BF16).reshape(ZS, z_rows, HEAD_DIM)
        for j in NEAREST[::-1]:
            gate_copy(j).start()
        gate_in[slot] = gate_out[z]

    for load in loads[9:]:
        load.wait()

    pairs = HEADS // 2
    steps = users * pairs

    def place_of(k):
        u, s = lax.div(k, pairs), lax.rem(k, pairs)
        early = lax.div(z, 2) + s + lax.div(s, 2) * (5 - 2 * s)
        late = x + 1 + s
        first = jnp.where(u == 0, 1, 0)
        return u, lax.rem(first * early + (1 - first) * late + 2 * pairs, pairs)

    def part_copy(u, p):
        j = lax.rem(p - x + XS, XS)
        return push(part.at[u, p], part_in.at[u, x], rx_s.at[u * XS + j], rx_r.at[u * XS + j],
                    p * ZS + z)

    def attend(k):
        u, p = place_of(k)
        heads = (2 * p, 2 * p + 1)

        for h in heads:
            @pl.when((k < pairs) & (h != z))
            def _():
                j = lax.rem(z - h + ZS, ZS)
                push(query.at[h], query.at[h], q_r.at[j], q_r.at[j], me).wait_recv()

        nothing = jnp.zeros((item_count, HEAD_DIM), BF16)
        asked = jnp.concatenate([
            jnp.concatenate([query[heads[0]], nothing], axis=1),
            jnp.concatenate([nothing, query[heads[1]]], axis=1)], axis=0)
        columns = pl.ds(pl.multiple_of(p * 2 * HEAD_DIM, 2 * HEAD_DIM), 2 * HEAD_DIM)
        scores = lax.dot_general(
            asked, keys[u, :, columns], (((1,), (1,)), ((), ())), preferred_element_type=F32)
        halved = scores * (0.5 * HEAD_DIM ** (-0.5))
        weight = halved + halved * jnp.tanh(halved)
        kept = jnp.concatenate(
            [(weight * live[u * tiles + t]).astype(BF16) for t in range(tiles)], axis=0)
        sums = jnp.dot(kept, vals[u, :, columns], preferred_element_type=F32)
        both = []
        for t in range(tiles):
            at = t * 2 * item_count
            both.append(jnp.concatenate([
                sums[at : at + item_count, :HEAD_DIM],
                sums[at + item_count : at + 2 * item_count, HEAD_DIM:]], axis=1))
        part[u, p] = jnp.dot(
            chooser[u], jnp.concatenate(both, axis=0).astype(BF16),
            preferred_element_type=F32).astype(BF16)

        @pl.when(p != x)
        def _():
            part_copy(u, p).start()

    def rows_z(at):
        return pl.ds(pl.multiple_of(at * z_rows, z_rows), z_rows)

    def half_copy(u, j):
        to = z_at(j)
        return push(half.at[u, rows_z(to)], half_in.at[u, z], rz_s.at[u * ZS + j], rz_r.at[u * ZS + j],
                    x * ZS + to)

    def reduce_x(u):
        total = part[u, x].astype(F32)
        for j in range(1, XS):
            come = part_in.at[u, x_at(-j)]
            push(come, come, rx_r.at[u * XS + j], rx_r.at[u * XS + j], me).wait_recv()
            total += part_in[u, x_at(-j)].astype(F32)
        half[u] = total.astype(BF16)
        for j in NEAREST[::-1]:
            half_copy(u, j).start()

    def project(u):
        attended = half[u, rows_z(z)].astype(F32)
        for j in NEAREST:
            come = half_in.at[u, z_at(-j)]
            push(come, come, rz_r.at[u * ZS + j], rz_r.at[u * ZS + j], me).wait_recv()
            attended += half_in[u, z_at(-j)].astype(F32)
        squares = attended * attended
        sq[u] = (squares[:, :HEAD_DIM] + squares[:, HEAD_DIM:]).reshape(XS, each, HEAD_DIM)
        gate = jnp.concatenate([gate_in[i, u] for i in range(HEADS // XS)], axis=1).astype(F32)
        width = 2 * HEAD_DIM
        gain = gain_attn[:, pl.ds(pl.multiple_of(x * width, width), width)]
        added = jnp.dot(
            (attended * gain * gate).astype(BF16), wo[...], preferred_element_type=F32
        ).reshape(XS, each, HEADS * HEAD_DIM)
        middle = HEADS * HEAD_DIM // 2
        proj[u] = jnp.concatenate([added[:, :, :middle], added[:, :, middle:]], axis=1).astype(BF16)
        for j in (2, 1, 3):
            to = x_at(j)
            send(push(proj.at[u, to], proj_in.at[u, x], po_s.at[u * XS + j], po_r.at[u * XS + j],
                      to * ZS + z))
            send(push(sq.at[u, to], sq_in.at[u, x], sq_s.at[u * XS + j], sq_r.at[u * XS + j],
                      to * ZS + z))

    def finish(u):
        squares = sq[u, x]
        projected = proj[u, x].astype(F32)
        for j in (1, 3, 2):
            frm = x_at(-j)
            push(proj_in.at[u, frm], proj_in.at[u, frm], po_r.at[u * XS + j], po_r.at[u * XS + j],
                 me).wait_recv()
            projected += proj_in[u, frm].astype(F32)
            push(sq_in.at[u, frm], sq_in.at[u, frm], sq_r.at[u * XS + j], sq_r.at[u * XS + j],
                 me).wait_recv()
            squares += sq_in[u, frm]
        scale = lax.rsqrt(
            jnp.sum(squares, axis=1, keepdims=True) * (1.0 / (HEADS * HEAD_DIM)) + EPSILON)
        projected = jnp.concatenate([projected[:each], projected[each:]], axis=1)
        return tokens[u * each : (u + 1) * each] + projected * scale

    def step(k, carry):
        attend(k)

        @pl.when(k == 2)
        def _():
            share_wo()

        @pl.when(k == steps - 2)
        def _():
            reduce_x(0)

        return carry

    lax.fori_loop(0, steps, step, 0)

    @pl.when(gate_x == x)
    def _():
        make_gate()

    for u in range(1, users):
        reduce_x(u)
    for i in range(HEADS // XS):
        frm = x * (HEADS // XS) + i

        @pl.when(frm != z)
        def _():
            push(gate_in.at[i], gate_in.at[i], ga_r.at[i], ga_r.at[i], me).wait_recv()
    loads[6].wait()
    for j in range(1, team):
        come = wo.at[:, share_of(lax.rem(member - j + team, team))]
        push(come, come, wo_tr.at[j], wo_tr.at[j], me).wait_recv()
    rows_out = []
    for u in range(users):
        project(u)
        rows_out.append(finish(u))
    out[...] = jnp.concatenate(rows_out, axis=0).astype(BF16)

    for copy in sends:
        copy.wait_send()
    for j in range(1, team):
        share_copy(j).wait_send()

    @pl.when(gate_x != x)
    def _():
        wg_copy.wait_send()

    @pl.when(gate_x == x)
    def _():
        for j in range(1, ZS):
            gate_copy(j).wait_send()

    for u in range(users):
        for j in range(1, XS):
            part_copy(u, x_at(j)).wait_send()
        for j in range(1, ZS):
            half_copy(u, j).wait_send()


def on_device(
    cand_items, item_rows, hist_keys, hist_values, block_mask, hist_lengths,
    gain_in, w_query, w_gate, gain_attn, w_out,
):
    row_count, users = cand_items.shape
    item_count, width = item_rows.shape
    events = hist_keys.shape[1]
    rows = w_query.shape[0]
    own = row_count * users
    tiles = block_mask.shape[1]
    user_rows = XS * ZS * row_count
    team = min(TEAM, lax.axis_size("users"))
    dma = pltpu.SemaphoreType.DMA
    anywhere = pl.BlockSpec(memory_space=pl.ANY)
    vmem = pl.BlockSpec(memory_space=pltpu.VMEM)
    ranked = pl.pallas_call(
        kernel,
        out_shape=jax.ShapeDtypeStruct((own, width), BF16),
        in_specs=[anywhere] * 11,
        out_specs=vmem,
        scratch_shapes=[
            pltpu.VMEM((users, row_count), jnp.int32),
            pltpu.SMEM(block_mask.shape, jnp.int32),
            pltpu.SMEM((users,), jnp.int32),
            pltpu.VMEM((1, width), F32),
            pltpu.VMEM((1, width), F32),
            pltpu.VMEM((item_count, width), BF16),
            pltpu.VMEM((users, events, width), BF16),
            pltpu.VMEM((users, events, width), BF16),
            pltpu.VMEM((item_count, width), BF16),
            pltpu.VMEM((ZS, own, item_count), BF16),
            pltpu.VMEM((XS, own, ZS * own), BF16),
            pltpu.VMEM((users, user_rows, tiles * item_count), BF16),
            pltpu.VMEM((users * tiles, 1, events), F32),
            pltpu.VMEM((own, width), F32),
            pltpu.VMEM((XS * ZS * rows, HEAD_DIM), BF16),
            pltpu.VMEM((XS * ZS * rows, HEAD_DIM), BF16),
            pltpu.VMEM((ZS * rows, width), BF16),
            pltpu.VMEM((HEADS, item_count, HEAD_DIM), BF16),
            pltpu.VMEM((ZS, users, user_rows // ZS, HEAD_DIM), BF16),
            pltpu.VMEM((HEADS // XS, users, user_rows // ZS, HEAD_DIM), BF16),
            pltpu.VMEM((users, XS, user_rows, 2 * HEAD_DIM), BF16),
            pltpu.VMEM((users, XS, user_rows, 2 * HEAD_DIM), BF16),
            pltpu.VMEM((users, user_rows, 2 * HEAD_DIM), BF16),
            pltpu.VMEM((users, ZS, user_rows // ZS, 2 * HEAD_DIM), BF16),
            pltpu.VMEM((users, XS, own, width // 2), BF16),
            pltpu.VMEM((users, XS, own, width // 2), BF16),
            pltpu.VMEM((users, XS, row_count, HEAD_DIM), F32),
            pltpu.VMEM((users, XS, row_count, HEAD_DIM), F32),
            dma((9 + 2 * users,)),
            dma((ZS,)), dma((ZS,)), dma((XS,)), dma((XS,)),
            dma((ZS,)), dma((ZS,)), dma((XS,)), dma((XS,)),
            dma((ZS,)), dma((ZS,)), dma((XS,)), dma((XS,)),
            dma((ZS,)), dma((ZS,)), dma((team,)), dma((team,)),
            dma((ZS,)), dma((ZS,)),
            dma((ZS,)), dma((HEADS // XS,)),
            dma((users * XS,)), dma((users * XS,)),
            dma((users * ZS,)), dma((users * ZS,)),
            dma((users * XS,)), dma((users * XS,)),
            dma((users * XS,)), dma((users * XS,)),
        ],
        compiler_params=pltpu.CompilerParams(
            collective_id=0, has_side_effects=True, vmem_limit_bytes=63 * 1024 * 1024),
        cost_estimate=pl.CostEstimate(flops=10**9, bytes_accessed=5 * 10**6, transcendentals=10**6),
        name="ranked",
    )(
        cand_items.T, item_rows, hist_keys, hist_values, block_mask, hist_lengths,
        gain_in.reshape(1, width), w_query, w_gate, gain_attn.reshape(1, width), w_out,
    )
    return ranked.reshape(users, row_count, width).transpose(1, 0, 2)


def solution(mesh):
    in_specs = (
        P(("users", "seq"), None),
        P("users", None),
        P("users", "seq", None),
        P("users", "seq", None),
        P("users", None, "seq"),
        P("users"),
        P(),
        P("seq", None),
        P("seq", None),
        P(),
        P("seq", None),
    )
    out_specs = P(("users", "seq"), None, None)
    return jax.shard_map(
        on_device, mesh=mesh, in_specs=in_specs, out_specs=out_specs, check_vma=False
    )
```

```python
import jax
import jax.numpy as jnp
from jax import lax
from jax.experimental import pallas as pl
from jax.experimental.pallas import tpu as pltpu
from jax.sharding import PartitionSpec as P

HEADS = 8
HEAD_DIM = 128
BLOCK = 128
EPSILON = 1e-06
XS, ZS = 4, 8
NEAREST = (7, 1, 6, 2, 5, 3, 4)
TEAM = 4
MESH = pl.DeviceIdType.MESH
BF16, F32 = jnp.bfloat16, jnp.float32


def silu(v):
    return v / (1.0 + jnp.exp(-v))


def push(src, dst, send_sem, recv_sem, seq):
    return pltpu.make_async_remote_copy(
        src_ref=src, dst_ref=dst, send_sem=send_sem, recv_sem=recv_sem,
        device_id={"seq": seq}, device_id_type=MESH)


def kernel(
    cand_hbm, items_hbm, keys_hbm, vals_hbm, mask_hbm, lens_hbm, gain_in_hbm, wq_hbm, wg_hbm,
    gain_attn_hbm, wo_hbm,
    out,
    cand, mask, lens, gain_in, gain_attn, items, keys, vals, normed, picks, ids_x, chooser, live,
    tokens, wq, query_part, wg, wo, query, gate_out, gate_in, part, part_in, half, half_in, proj, proj_in, sq, sq_in,
    load_sem, wq_zs, wq_zr, wq_xs, wq_xr, wg_zs, wg_zr, wg_xs, wg_xr, oh_zs, oh_zr, oh_xs, oh_xr,
    wo_zs, wo_zr, wo_ts, wo_tr, q_s, q_r, ga_s, ga_r, rx_s, rx_r, rz_s, rz_r, po_s, po_r, sq_s, sq_r,
):
    me = lax.axis_index("seq")
    x, z = lax.div(me, ZS), lax.rem(me, ZS)
    team = min(TEAM, lax.axis_size("users"))
    member = lax.rem(lax.axis_index("users"), team)
    team_at = lax.axis_index("users") - member
    rows = wq_hbm.shape[0]
    own = picks.shape[1]
    tiles = mask.shape[1]
    users, events = keys_hbm.shape[0], keys_hbm.shape[1]
    item_count = items_hbm.shape[0]

    def z_at(step):
        return lax.rem(z + step + ZS, ZS)

    def x_at(step):
        return lax.rem(x + step + XS, XS)

    def lanes(index):
        return pl.ds(pl.multiple_of(index * HEAD_DIM, HEAD_DIM), HEAD_DIM)

    def rows_of(seq):
        return pl.ds(pl.multiple_of(seq * rows, rows), rows)

    share = wo_hbm.shape[1] // team

    def share_of(at):
        return pl.ds(pl.multiple_of(at * share, share), share)

    def mate(step):
        return lax.rem(member + step, team)

    barrier = pltpu.get_barrier_semaphore()
    for j in range(1, ZS):
        pl.semaphore_signal(barrier, inc=1, device_id={"seq": x * ZS + z_at(j)}, device_id_type=MESH)
    for j in range(1, XS):
        pl.semaphore_signal(barrier, inc=1, device_id={"seq": x_at(j) * ZS + z}, device_id_type=MESH)

    for j in range(1, team):
        pl.semaphore_signal(barrier, inc=1, device_id={"users": team_at + mate(j)}, device_id_type=MESH)

    loads = [
        pltpu.make_async_copy(cand_hbm, cand, load_sem.at[0]),
        pltpu.make_async_copy(items_hbm, items, load_sem.at[1]),
        pltpu.make_async_copy(gain_in_hbm, gain_in, load_sem.at[2]),
        pltpu.make_async_copy(wq_hbm.at[:, lanes(z)], wq.at[rows_of(me)], load_sem.at[3]),
        pltpu.make_async_copy(wg_hbm.at[:, lanes(z)], wg.at[rows_of(me)], load_sem.at[4]),
        pltpu.make_async_copy(
            wo_hbm.at[:, share_of(member)], wo.at[rows_of(z), share_of(member)], load_sem.at[5]),
        pltpu.make_async_copy(gain_attn_hbm, gain_attn, load_sem.at[6]),
        pltpu.make_async_copy(mask_hbm, mask, load_sem.at[7]),
        pltpu.make_async_copy(lens_hbm, lens, load_sem.at[8]),
    ]
    for u in range(users):
        loads.append(pltpu.make_async_copy(keys_hbm.at[u], keys.at[u], load_sem.at[9 + 2 * u]))
        loads.append(pltpu.make_async_copy(vals_hbm.at[u], vals.at[u], load_sem.at[10 + 2 * u]))
    for load in loads[:4]:
        load.start()

    pl.semaphore_wait(barrier, XS + ZS + team - 3)

    sends = []

    def send(copy):
        copy.start()
        sends.append(copy)

    for j in range(1, ZS):
        to = z_at(j)
        send(push(wq_hbm.at[:, lanes(to)], wq.at[rows_of(me)], wq_zs.at[j], wq_zr.at[j], x * ZS + to))
    for load in loads[4:]:
        load.start()

    loads[0].wait()
    each = own // users
    row = lax.broadcasted_iota(jnp.int32, (own, each), 0)
    column = lax.broadcasted_iota(jnp.int32, (own, each), 1)
    ids = jnp.zeros((own, 1), F32)
    for u in range(users):
        here = row == column + u * each
        ids += jnp.sum(
            jnp.where(here, cand[u : u + 1, :].astype(F32), 0.0), axis=1, keepdims=True)
    item = lax.broadcasted_iota(jnp.int32, (own, item_count), 1).astype(F32)
    own_pick = jnp.where(item == ids, 1.0, 0.0).astype(BF16)
    picks[z] = own_pick

    for j in range(1, ZS):
        send(push(picks.at[z], picks.at[z], oh_zs.at[j], oh_zr.at[j], x * ZS + z_at(j)))

    loads[1].wait()
    loads[2].wait()
    wide = items[...].astype(F32)
    normed[...] = (
        wide * lax.rsqrt(jnp.mean(wide * wide, axis=-1, keepdims=True) + EPSILON) * gain_in[...]
    ).astype(BF16)

    def group(at):
        return pl.ds(pl.multiple_of(at * (ZS * rows), ZS * rows), ZS * rows)

    loads[3].wait()
    for j in range(1, ZS):
        come = wq.at[rows_of(x * ZS + z_at(-j))]
        push(come, come, wq_zr.at[j], wq_zr.at[j], me).wait_recv()
    depth = ZS * rows
    own_part = jnp.dot(
        normed[:, pl.ds(pl.multiple_of(x * depth, depth), depth)], wq[group(x)],
        preferred_element_type=F32)
    query_part[x] = own_part.astype(BF16)
    for j in range(1, XS):
        send(push(query_part.at[x], query_part.at[x], wq_xs.at[j], wq_xr.at[j], x_at(j) * ZS + z))

    for j in range(1, ZS):
        to = z_at(j)
        send(push(wg_hbm.at[:, lanes(to)], wg.at[rows_of(me)], wg_zs.at[j], wg_zr.at[j], x * ZS + to))

    for j in range(1, ZS):
        come = picks.at[z_at(-j)]
        push(come, come, oh_zr.at[j], oh_zr.at[j], me).wait_recv()
    group_rows = ZS * own
    picked = picks[...].reshape(group_rows, item_count)
    number = lax.broadcasted_iota(jnp.int32, (own, item_count), 1).astype(F32).astype(BF16)
    ids_x[x] = lax.dot_general(
        number, picked, (((1,), (1,)), ((), ())), preferred_element_type=F32).astype(BF16)
    for j in range(1, XS):
        send(push(ids_x.at[x], ids_x.at[x], oh_xs.at[j], oh_xr.at[j], x_at(j) * ZS + z))

    tokens[...] = jnp.dot(own_pick, items[...], preferred_element_type=F32)
    loads[7].wait()
    loads[8].wait()
    for u in range(users):
        length = lens[u] - me * events
        for t in range(tiles):
            for b in range(events // BLOCK):
                place = b * BLOCK + lax.broadcasted_iota(jnp.int32, (1, BLOCK), 1)
                opened = jnp.full((1, BLOCK), mask[u, t, b], jnp.int32)
                live[u * tiles + t, :, pl.ds(b * BLOCK, BLOCK)] = jnp.where(
                    (opened == 1) & (place < length), 1.0, 0.0)

    asked_z = own_part
    for j in range(1, XS):
        come = query_part.at[x_at(-j)]
        push(come, come, wq_xr.at[j], wq_xr.at[j], me).wait_recv()
        asked_z += query_part[x_at(-j)].astype(F32)
    query[z] = silu(asked_z).astype(BF16)
    for j in NEAREST:
        send(push(query.at[z], query.at[z], q_s.at[j], q_r.at[j], x * ZS + z_at(j)))

    gate_x = lax.div(z, HEADS // XS)
    gate_step = lax.rem(gate_x - x + XS, XS)
    wg_copy = push(wg.at[group(x)], wg.at[group(x)], wg_xs.at[gate_step], wg_xr.at[gate_step],
                   gate_x * ZS + z)
    slot = lax.rem(z, HEADS // XS)
    loads[4].wait()
    for j in range(1, ZS):
        come = wg.at[rows_of(x * ZS + z_at(-j))]
        push(come, come, wg_zr.at[j], wg_zr.at[j], me).wait_recv()

    @pl.when(gate_x != x)
    def _():
        wg_copy.start()

    for j in range(1, ZS):
        send(push(wo_hbm.at[:, share_of(member)], wo.at[rows_of(z), share_of(member)],
                  wo_zs.at[j], wo_zr.at[j], x * ZS + z_at(j)))

    def share_copy(j):
        return pltpu.make_async_remote_copy(
            src_ref=wo.at[:, share_of(member)], dst_ref=wo.at[:, share_of(member)],
            send_sem=wo_ts.at[j], recv_sem=wo_tr.at[j],
            device_id={"users": team_at + mate(j)}, device_id_type=MESH)

    def share_wo():
        loads[5].wait()
        for j in range(1, ZS):
            come = wo.at[rows_of(z_at(-j)), share_of(member)]
            push(come, come, wo_zr.at[j], wo_zr.at[j], me).wait_recv()
        for j in range(1, team):
            share_copy(j).start()

    for j in range(1, XS):
        come = ids_x.at[x_at(-j)]
        push(come, come, oh_xr.at[j], oh_xr.at[j], me).wait_recv()
    down = lax.broadcasted_iota(jnp.int32, (item_count, group_rows), 0).astype(F32)
    per_tile = XS // tiles
    user_rows = XS * ZS * each
    z_rows = XS * each
    shown = []
    for s in range(XS):
        chosen = jnp.transpose(jnp.where(down == ids_x[s, 0:1, :].astype(F32), 1.0, 0.0))
        shown.append(chosen.reshape(ZS, own, item_count))
    blank = jnp.zeros((ZS, each, item_count), F32)
    for u in range(users):
        wide_rows = []
        for s in range(XS):
            mine = shown[s][:, u * each : (u + 1) * each]
            wide_rows.append(jnp.concatenate(
                [mine if t == s // per_tile else blank for t in range(tiles)], axis=2))
        chooser[u] = jnp.concatenate(wide_rows, axis=1).reshape(
            user_rows, tiles * item_count).astype(BF16)

    def gate_copy(j):
        to = z_at(j)
        return push(gate_out.at[to], gate_in.at[slot], ga_s.at[j], ga_r.at[slot], x * ZS + to)

    def make_gate():
        for j in range(1, XS):
            come = wg.at[group(x_at(-j))]
            push(come, come, wg_xr.at[j], wg_xr.at[j], me).wait_recv()
        gate_items = silu(jnp.dot(normed[...], wg[...], preferred_element_type=F32)).astype(BF16)
        twice = jnp.concatenate([gate_items] * tiles, axis=0)
        for u in range(users):
            gate_out[:, u] = jnp.dot(
                chooser[u], twice, preferred_element_type=F32
            ).astype(BF16).reshape(ZS, z_rows, HEAD_DIM)
        for j in NEAREST[::-1]:
            gate_copy(j).start()
        gate_in[slot] = gate_out[z]

    for load in loads[9:]:
        load.wait()

    pairs = HEADS // 2
    steps = users * pairs

    def place_of(k):
        u, s = lax.div(k, pairs), lax.rem(k, pairs)
        early = lax.div(z, 2) + s + lax.div(s, 2) * (5 - 2 * s)
        late = x + 1 + s
        first = jnp.where(u == 0, 1, 0)
        return u, lax.rem(first * early + (1 - first) * late + 2 * pairs, pairs)

    def part_copy(u, p):
        j = lax.rem(p - x + XS, XS)
        return push(part.at[u, p], part_in.at[u, x], rx_s.at[u * XS + j], rx_r.at[u * XS + j],
                    p * ZS + z)

    def attend(k):
        u, p = place_of(k)
        heads = (2 * p, 2 * p + 1)

        for h in heads:
            @pl.when((k < pairs) & (h != z))
            def _():
                j = lax.rem(z - h + ZS, ZS)
                push(query.at[h], query.at[h], q_r.at[j], q_r.at[j], me).wait_recv()

        nothing = jnp.zeros((item_count, HEAD_DIM), BF16)
        asked = jnp.concatenate([
            jnp.concatenate([query[heads[0]], nothing], axis=1),
            jnp.concatenate([nothing, query[heads[1]]], axis=1)], axis=0)
        columns = pl.ds(pl.multiple_of(p * 2 * HEAD_DIM, 2 * HEAD_DIM), 2 * HEAD_DIM)
        scores = lax.dot_general(
            asked, keys[u, :, columns], (((1,), (1,)), ((), ())), preferred_element_type=F32)
        halved = scores * (0.5 * HEAD_DIM ** (-0.5))
        weight = halved + halved * jnp.tanh(halved)
        kept = jnp.concatenate(
            [(weight * live[u * tiles + t]).astype(BF16) for t in range(tiles)], axis=0)
        sums = jnp.dot(kept, vals[u, :, columns], preferred_element_type=F32)
        both = []
        for t in range(tiles):
            at = t * 2 * item_count
            both.append(jnp.concatenate([
                sums[at : at + item_count, :HEAD_DIM],
                sums[at + item_count : at + 2 * item_count, HEAD_DIM:]], axis=1))
        part[u, p] = jnp.dot(
            chooser[u], jnp.concatenate(both, axis=0).astype(BF16),
            preferred_element_type=F32).astype(BF16)

        @pl.when(p != x)
        def _():
            part_copy(u, p).start()

    def rows_z(at):
        return pl.ds(pl.multiple_of(at * z_rows, z_rows), z_rows)

    def half_copy(u, j):
        to = z_at(j)
        return push(half.at[u, rows_z(to)], half_in.at[u, z], rz_s.at[u * ZS + j], rz_r.at[u * ZS + j],
                    x * ZS + to)

    def reduce_x(u):
        total = part[u, x].astype(F32)
        for j in range(1, XS):
            come = part_in.at[u, x_at(-j)]
            push(come, come, rx_r.at[u * XS + j], rx_r.at[u * XS + j], me).wait_recv()
            total += part_in[u, x_at(-j)].astype(F32)
        half[u] = total.astype(BF16)
        for j in NEAREST[::-1]:
            half_copy(u, j).start()

    def project(u):
        attended = half[u, rows_z(z)].astype(F32)
        for j in NEAREST:
            come = half_in.at[u, z_at(-j)]
            push(come, come, rz_r.at[u * ZS + j], rz_r.at[u * ZS + j], me).wait_recv()
            attended += half_in[u, z_at(-j)].astype(F32)
        squares = attended * attended
        sq[u] = (squares[:, :HEAD_DIM] + squares[:, HEAD_DIM:]).reshape(XS, each, HEAD_DIM)
        gate = jnp.concatenate([gate_in[i, u] for i in range(HEADS // XS)], axis=1).astype(F32)
        width = 2 * HEAD_DIM
        gain = gain_attn[:, pl.ds(pl.multiple_of(x * width, width), width)]
        added = jnp.dot(
            (attended * gain * gate).astype(BF16), wo[...], preferred_element_type=F32
        ).reshape(XS, each, HEADS * HEAD_DIM)
        middle = HEADS * HEAD_DIM // 2
        proj[u] = jnp.concatenate([added[:, :, :middle], added[:, :, middle:]], axis=1).astype(BF16)
        for j in (2, 1, 3):
            to = x_at(j)
            send(push(proj.at[u, to], proj_in.at[u, x], po_s.at[u * XS + j], po_r.at[u * XS + j],
                      to * ZS + z))
            send(push(sq.at[u, to], sq_in.at[u, x], sq_s.at[u * XS + j], sq_r.at[u * XS + j],
                      to * ZS + z))

    def finish(u):
        squares = sq[u, x]
        projected = proj[u, x].astype(F32)
        for j in (1, 3, 2):
            frm = x_at(-j)
            push(proj_in.at[u, frm], proj_in.at[u, frm], po_r.at[u * XS + j], po_r.at[u * XS + j],
                 me).wait_recv()
            projected += proj_in[u, frm].astype(F32)
            push(sq_in.at[u, frm], sq_in.at[u, frm], sq_r.at[u * XS + j], sq_r.at[u * XS + j],
                 me).wait_recv()
            squares += sq_in[u, frm]
        scale = lax.rsqrt(
            jnp.sum(squares, axis=1, keepdims=True) * (1.0 / (HEADS * HEAD_DIM)) + EPSILON)
        projected = jnp.concatenate([projected[:each], projected[each:]], axis=1)
        return tokens[u * each : (u + 1) * each] + projected * scale

    def step(k, carry):
        attend(k)

        @pl.when((k == 1) & (gate_x == x))
        def _():
            make_gate()

        @pl.when(k == steps - 2)
        def _():
            reduce_x(0)
            share_wo()

        return carry

    lax.fori_loop(0, steps, step, 0)
    for u in range(1, users):
        reduce_x(u)
    for i in range(HEADS // XS):
        frm = x * (HEADS // XS) + i

        @pl.when(frm != z)
        def _():
            push(gate_in.at[i], gate_in.at[i], ga_r.at[i], ga_r.at[i], me).wait_recv()
    loads[6].wait()
    for j in range(1, team):
        come = wo.at[:, share_of(lax.rem(member - j + team, team))]
        push(come, come, wo_tr.at[j], wo_tr.at[j], me).wait_recv()
    for u in range(users):
        project(u)
    rows_out = [finish(u) for u in range(users)]
    out[...] = jnp.concatenate(rows_out, axis=0).astype(BF16)

    for copy in sends:
        copy.wait_send()
    for j in range(1, team):
        share_copy(j).wait_send()

    @pl.when(gate_x != x)
    def _():
        wg_copy.wait_send()

    @pl.when(gate_x == x)
    def _():
        for j in range(1, ZS):
            gate_copy(j).wait_send()

    for u in range(users):
        for j in range(1, XS):
            part_copy(u, x_at(j)).wait_send()
        for j in range(1, ZS):
            half_copy(u, j).wait_send()


def on_device(
    cand_items, item_rows, hist_keys, hist_values, block_mask, hist_lengths,
    gain_in, w_query, w_gate, gain_attn, w_out,
):
    row_count, users = cand_items.shape
    item_count, width = item_rows.shape
    events = hist_keys.shape[1]
    rows = w_query.shape[0]
    own = row_count * users
    tiles = block_mask.shape[1]
    user_rows = XS * ZS * row_count
    team = min(TEAM, lax.axis_size("users"))
    dma = pltpu.SemaphoreType.DMA
    anywhere = pl.BlockSpec(memory_space=pl.ANY)
    vmem = pl.BlockSpec(memory_space=pltpu.VMEM)
    ranked = pl.pallas_call(
        kernel,
        out_shape=jax.ShapeDtypeStruct((own, width), BF16),
        in_specs=[anywhere] * 11,
        out_specs=vmem,
        scratch_shapes=[
            pltpu.VMEM((users, row_count), jnp.int32),
            pltpu.SMEM(block_mask.shape, jnp.int32),
            pltpu.SMEM((users,), jnp.int32),
            pltpu.VMEM((1, width), F32),
            pltpu.VMEM((1, width), F32),
            pltpu.VMEM((item_count, width), BF16),
            pltpu.VMEM((users, events, width), BF16),
            pltpu.VMEM((users, events, width), BF16),
            pltpu.VMEM((item_count, width), BF16),
            pltpu.VMEM((ZS, own, item_count), BF16),
            pltpu.VMEM((XS, own, ZS * own), BF16),
            pltpu.VMEM((users, user_rows, tiles * item_count), BF16),
            pltpu.VMEM((users * tiles, 1, events), F32),
            pltpu.VMEM((own, width), F32),
            pltpu.VMEM((XS * ZS * rows, HEAD_DIM), BF16),
            pltpu.VMEM((XS, item_count, HEAD_DIM), BF16),
            pltpu.VMEM((XS * ZS * rows, HEAD_DIM), BF16),
            pltpu.VMEM((ZS * rows, width), BF16),
            pltpu.VMEM((HEADS, item_count, HEAD_DIM), BF16),
            pltpu.VMEM((ZS, users, user_rows // ZS, HEAD_DIM), BF16),
            pltpu.VMEM((HEADS // XS, users, user_rows // ZS, HEAD_DIM), BF16),
            pltpu.VMEM((users, XS, user_rows, 2 * HEAD_DIM), BF16),
            pltpu.VMEM((users, XS, user_rows, 2 * HEAD_DIM), BF16),
            pltpu.VMEM((users, user_rows, 2 * HEAD_DIM), BF16),
            pltpu.VMEM((users, ZS, user_rows // ZS, 2 * HEAD_DIM), BF16),
            pltpu.VMEM((users, XS, own, width // 2), BF16),
            pltpu.VMEM((users, XS, own, width // 2), BF16),
            pltpu.VMEM((users, XS, row_count, HEAD_DIM), F32),
            pltpu.VMEM((users, XS, row_count, HEAD_DIM), F32),
            dma((9 + 2 * users,)),
            dma((ZS,)), dma((ZS,)), dma((XS,)), dma((XS,)),
            dma((ZS,)), dma((ZS,)), dma((XS,)), dma((XS,)),
            dma((ZS,)), dma((ZS,)), dma((XS,)), dma((XS,)),
            dma((ZS,)), dma((ZS,)), dma((team,)), dma((team,)),
            dma((ZS,)), dma((ZS,)),
            dma((ZS,)), dma((HEADS // XS,)),
            dma((users * XS,)), dma((users * XS,)),
            dma((users * ZS,)), dma((users * ZS,)),
            dma((users * XS,)), dma((users * XS,)),
            dma((users * XS,)), dma((users * XS,)),
        ],
        compiler_params=pltpu.CompilerParams(
            collective_id=0, has_side_effects=True, vmem_limit_bytes=63 * 1024 * 1024),
        cost_estimate=pl.CostEstimate(flops=10**9, bytes_accessed=5 * 10**6, transcendentals=10**6),
        name="ranked",
    )(
        cand_items.T, item_rows, hist_keys, hist_values, block_mask, hist_lengths,
        gain_in.reshape(1, width), w_query, w_gate, gain_attn.reshape(1, width), w_out,
    )
    return ranked.reshape(users, row_count, width).transpose(1, 0, 2)


def solution(mesh):
    in_specs = (
        P(("users", "seq"), None),
        P("users", None),
        P("users", "seq", None),
        P("users", "seq", None),
        P("users", None, "seq"),
        P("users"),
        P(),
        P("seq", None),
        P("seq", None),
        P(),
        P("seq", None),
    )
    out_specs = P(("users", "seq"), None, None)
    return jax.shard_map(
        on_device, mesh=mesh, in_specs=in_specs, out_specs=out_specs, check_vma=False
    )
```

```python
import jax
import jax.numpy as jnp
from jax import lax
from jax.experimental import pallas as pl
from jax.experimental.pallas import tpu as pltpu
from jax.sharding import PartitionSpec as P

HEADS = 8
HEAD_DIM = 128
BLOCK = 128
EPSILON = 1e-06
XS, ZS = 4, 8
NEAREST = (7, 1, 6, 2, 5, 3, 4)
TEAM = 2
MESH = pl.DeviceIdType.MESH
BF16, F32 = jnp.bfloat16, jnp.float32


def silu(v):
    return v / (1.0 + jnp.exp(-v))


def push(src, dst, send_sem, recv_sem, seq):
    return pltpu.make_async_remote_copy(
        src_ref=src, dst_ref=dst, send_sem=send_sem, recv_sem=recv_sem,
        device_id={"seq": seq}, device_id_type=MESH)


def kernel(
    cand_hbm, items_hbm, keys_hbm, vals_hbm, mask_hbm, lens_hbm, gain_in_hbm, wq_hbm, wg_hbm,
    gain_attn_hbm, wo_hbm,
    out,
    cand, mask, lens, gain_in, gain_attn, items, keys, vals, normed, picks, ids_x, chooser, live,
    tokens, wq, query_part, wg, wo, query, gate_out, gate_in, part, part_in, half, half_in, proj, proj_in, sq, sq_in,
    load_sem, wq_zs, wq_zr, wq_xs, wq_xr, wg_zs, wg_zr, wg_xs, wg_xr, oh_zs, oh_zr, oh_xs, oh_xr,
    wo_zs, wo_zr, wo_ts, wo_tr, q_s, q_r, ga_s, ga_r, rx_s, rx_r, rz_s, rz_r, po_s, po_r, sq_s, sq_r,
):
    me = lax.axis_index("seq")
    x, z = lax.div(me, ZS), lax.rem(me, ZS)
    team = min(TEAM, lax.axis_size("users"))
    member = lax.rem(lax.axis_index("users"), team)
    team_at = lax.axis_index("users") - member
    rows = wq_hbm.shape[0]
    own = picks.shape[1]
    tiles = mask.shape[1]
    users, events = keys_hbm.shape[0], keys_hbm.shape[1]
    item_count = items_hbm.shape[0]

    def z_at(step):
        return lax.rem(z + step + ZS, ZS)

    def x_at(step):
        return lax.rem(x + step + XS, XS)

    def lanes(index):
        return pl.ds(pl.multiple_of(index * HEAD_DIM, HEAD_DIM), HEAD_DIM)

    def rows_of(seq):
        return pl.ds(pl.multiple_of(seq * rows, rows), rows)

    share = wo_hbm.shape[1] // team

    def share_of(at):
        return pl.ds(pl.multiple_of(at * share, share), share)

    def mate(step):
        return lax.rem(member + step, team)

    barrier = pltpu.get_barrier_semaphore()
    for j in range(1, ZS):
        pl.semaphore_signal(barrier, inc=1, device_id={"seq": x * ZS + z_at(j)}, device_id_type=MESH)
    for j in range(1, XS):
        pl.semaphore_signal(barrier, inc=1, device_id={"seq": x_at(j) * ZS + z}, device_id_type=MESH)

    for j in range(1, team):
        pl.semaphore_signal(barrier, inc=1, device_id={"users": team_at + mate(j)}, device_id_type=MESH)

    loads = [
        pltpu.make_async_copy(cand_hbm, cand, load_sem.at[0]),
        pltpu.make_async_copy(items_hbm, items, load_sem.at[1]),
        pltpu.make_async_copy(gain_in_hbm, gain_in, load_sem.at[2]),
        pltpu.make_async_copy(wq_hbm.at[:, lanes(z)], wq.at[rows_of(me)], load_sem.at[3]),
        pltpu.make_async_copy(wg_hbm.at[:, lanes(z)], wg.at[rows_of(me)], load_sem.at[4]),
        pltpu.make_async_copy(
            wo_hbm.at[:, share_of(member)], wo.at[rows_of(z), share_of(member)], load_sem.at[5]),
        pltpu.make_async_copy(gain_attn_hbm, gain_attn, load_sem.at[6]),
        pltpu.make_async_copy(mask_hbm, mask, load_sem.at[7]),
        pltpu.make_async_copy(lens_hbm, lens, load_sem.at[8]),
    ]
    for u in range(users):
        loads.append(pltpu.make_async_copy(keys_hbm.at[u], keys.at[u], load_sem.at[9 + 2 * u]))
        loads.append(pltpu.make_async_copy(vals_hbm.at[u], vals.at[u], load_sem.at[10 + 2 * u]))
    for load in loads[:4]:
        load.start()

    pl.semaphore_wait(barrier, XS + ZS + team - 3)

    sends = []

    def send(copy):
        copy.start()
        sends.append(copy)

    for j in range(1, ZS):
        to = z_at(j)
        send(push(wq_hbm.at[:, lanes(to)], wq.at[rows_of(me)], wq_zs.at[j], wq_zr.at[j], x * ZS + to))
    for load in loads[4:]:
        load.start()

    loads[0].wait()
    each = own // users
    row = lax.broadcasted_iota(jnp.int32, (own, each), 0)
    column = lax.broadcasted_iota(jnp.int32, (own, each), 1)
    ids = jnp.zeros((own, 1), F32)
    for u in range(users):
        here = row == column + u * each
        ids += jnp.sum(
            jnp.where(here, cand[u : u + 1, :].astype(F32), 0.0), axis=1, keepdims=True)
    item = lax.broadcasted_iota(jnp.int32, (own, item_count), 1).astype(F32)
    own_pick = jnp.where(item == ids, 1.0, 0.0).astype(BF16)
    picks[z] = own_pick

    for j in range(1, ZS):
        send(push(picks.at[z], picks.at[z], oh_zs.at[j], oh_zr.at[j], x * ZS + z_at(j)))

    loads[1].wait()
    loads[2].wait()
    wide = items[...].astype(F32)
    normed[...] = (
        wide * lax.rsqrt(jnp.mean(wide * wide, axis=-1, keepdims=True) + EPSILON) * gain_in[...]
    ).astype(BF16)

    def group(at):
        return pl.ds(pl.multiple_of(at * (ZS * rows), ZS * rows), ZS * rows)

    loads[3].wait()
    for j in range(1, ZS):
        come = wq.at[rows_of(x * ZS + z_at(-j))]
        push(come, come, wq_zr.at[j], wq_zr.at[j], me).wait_recv()
    depth = ZS * rows
    own_part = jnp.dot(
        normed[:, pl.ds(pl.multiple_of(x * depth, depth), depth)], wq[group(x)],
        preferred_element_type=F32)
    query_part[x] = own_part.astype(BF16)
    for j in range(1, XS):
        send(push(query_part.at[x], query_part.at[x], wq_xs.at[j], wq_xr.at[j], x_at(j) * ZS + z))

    for j in range(1, ZS):
        to = z_at(j)
        send(push(wg_hbm.at[:, lanes(to)], wg.at[rows_of(me)], wg_zs.at[j], wg_zr.at[j], x * ZS + to))

    for j in range(1, ZS):
        come = picks.at[z_at(-j)]
        push(come, come, oh_zr.at[j], oh_zr.at[j], me).wait_recv()
    group_rows = ZS * own
    picked = picks[...].reshape(group_rows, item_count)
    number = lax.broadcasted_iota(jnp.int32, (own, item_count), 1).astype(F32).astype(BF16)
    ids_x[x] = lax.dot_general(
        number, picked, (((1,), (1,)), ((), ())), preferred_element_type=F32).astype(BF16)
    for j in range(1, XS):
        send(push(ids_x.at[x], ids_x.at[x], oh_xs.at[j], oh_xr.at[j], x_at(j) * ZS + z))

    tokens[...] = jnp.dot(own_pick, items[...], preferred_element_type=F32)
    loads[7].wait()
    loads[8].wait()
    for u in range(users):
        length = lens[u] - me * events
        for t in range(tiles):
            for b in range(events // BLOCK):
                place = b * BLOCK + lax.broadcasted_iota(jnp.int32, (1, BLOCK), 1)
                opened = jnp.full((1, BLOCK), mask[u, t, b], jnp.int32)
                live[u * tiles + t, :, pl.ds(b * BLOCK, BLOCK)] = jnp.where(
                    (opened == 1) & (place < length), 1.0, 0.0)

    asked_z = own_part
    for j in range(1, XS):
        come = query_part.at[x_at(-j)]
        push(come, come, wq_xr.at[j], wq_xr.at[j], me).wait_recv()
        asked_z += query_part[x_at(-j)].astype(F32)
    query[z] = silu(asked_z).astype(BF16)
    for j in NEAREST:
        send(push(query.at[z], query.at[z], q_s.at[j], q_r.at[j], x * ZS + z_at(j)))

    gate_x = lax.div(z, HEADS // XS)
    gate_step = lax.rem(gate_x - x + XS, XS)
    wg_copy = push(wg.at[group(x)], wg.at[group(x)], wg_xs.at[gate_step], wg_xr.at[gate_step],
                   gate_x * ZS + z)
    slot = lax.rem(z, HEADS // XS)
    loads[4].wait()
    for j in range(1, ZS):
        come = wg.at[rows_of(x * ZS + z_at(-j))]
        push(come, come, wg_zr.at[j], wg_zr.at[j], me).wait_recv()

    @pl.when(gate_x != x)
    def _():
        wg_copy.start()

    for j in range(1, ZS):
        send(push(wo_hbm.at[:, share_of(member)], wo.at[rows_of(z), share_of(member)],
                  wo_zs.at[j], wo_zr.at[j], x * ZS + z_at(j)))

    def share_copy(j):
        return pltpu.make_async_remote_copy(
            src_ref=wo.at[:, share_of(member)], dst_ref=wo.at[:, share_of(member)],
            send_sem=wo_ts.at[j], recv_sem=wo_tr.at[j],
            device_id={"users": team_at + mate(j)}, device_id_type=MESH)

    def share_wo():
        loads[5].wait()
        for j in range(1, ZS):
            come = wo.at[rows_of(z_at(-j)), share_of(member)]
            push(come, come, wo_zr.at[j], wo_zr.at[j], me).wait_recv()
        for j in range(1, team):
            share_copy(j).start()

    for j in range(1, XS):
        come = ids_x.at[x_at(-j)]
        push(come, come, oh_xr.at[j], oh_xr.at[j], me).wait_recv()
    down = lax.broadcasted_iota(jnp.int32, (item_count, group_rows), 0).astype(F32)
    per_tile = XS // tiles
    user_rows = XS * ZS * each
    z_rows = XS * each
    shown = []
    for s in range(XS):
        chosen = jnp.transpose(jnp.where(down == ids_x[s, 0:1, :].astype(F32), 1.0, 0.0))
        shown.append(chosen.reshape(ZS, own, item_count))
    blank = jnp.zeros((ZS, each, item_count), F32)
    for u in range(users):
        wide_rows = []
        for s in range(XS):
            mine = shown[s][:, u * each : (u + 1) * each]
            wide_rows.append(jnp.concatenate(
                [mine if t == s // per_tile else blank for t in range(tiles)], axis=2))
        chooser[u] = jnp.concatenate(wide_rows, axis=1).reshape(
            user_rows, tiles * item_count).astype(BF16)

    def gate_copy(j):
        to = z_at(j)
        return push(gate_out.at[to], gate_in.at[slot], ga_s.at[j], ga_r.at[slot], x * ZS + to)

    def make_gate():
        for j in range(1, XS):
            come = wg.at[group(x_at(-j))]
            push(come, come, wg_xr.at[j], wg_xr.at[j], me).wait_recv()
        gate_items = silu(jnp.dot(normed[...], wg[...], preferred_element_type=F32)).astype(BF16)
        twice = jnp.concatenate([gate_items] * tiles, axis=0)
        for u in range(users):
            gate_out[:, u] = jnp.dot(
                chooser[u], twice, preferred_element_type=F32
            ).astype(BF16).reshape(ZS, z_rows, HEAD_DIM)
        for j in NEAREST[::-1]:
            gate_copy(j).start()
        gate_in[slot] = gate_out[z]

    for load in loads[9:]:
        load.wait()

    pairs = HEADS // 2
    steps = users * pairs

    def place_of(k):
        u, s = lax.div(k, pairs), lax.rem(k, pairs)
        early = lax.div(z, 2) + s + lax.div(s, 2) * (5 - 2 * s)
        late = x + 1 + s
        first = jnp.where(u == 0, 1, 0)
        return u, lax.rem(first * early + (1 - first) * late + 2 * pairs, pairs)

    def part_copy(u, p):
        j = lax.rem(p - x + XS, XS)
        return push(part.at[u, p], part_in.at[u, x], rx_s.at[u * XS + j], rx_r.at[u * XS + j],
                    p * ZS + z)

    def attend(k):
        u, p = place_of(k)
        heads = (2 * p, 2 * p + 1)

        for h in heads:
            @pl.when((k < pairs) & (h != z))
            def _():
                j = lax.rem(z - h + ZS, ZS)
                push(query.at[h], query.at[h], q_r.at[j], q_r.at[j], me).wait_recv()

        nothing = jnp.zeros((item_count, HEAD_DIM), BF16)
        asked = jnp.concatenate([
            jnp.concatenate([query[heads[0]], nothing], axis=1),
            jnp.concatenate([nothing, query[heads[1]]], axis=1)], axis=0)
        columns = pl.ds(pl.multiple_of(p * 2 * HEAD_DIM, 2 * HEAD_DIM), 2 * HEAD_DIM)
        scores = lax.dot_general(
            asked, keys[u, :, columns], (((1,), (1,)), ((), ())), preferred_element_type=F32)
        halved = scores * (0.5 * HEAD_DIM ** (-0.5))
        weight = halved + halved * jnp.tanh(halved)
        kept = jnp.concatenate(
            [(weight * live[u * tiles + t]).astype(BF16) for t in range(tiles)], axis=0)
        sums = jnp.dot(kept, vals[u, :, columns], preferred_element_type=F32)
        both = []
        for t in range(tiles):
            at = t * 2 * item_count
            both.append(jnp.concatenate([
                sums[at : at + item_count, :HEAD_DIM],
                sums[at + item_count : at + 2 * item_count, HEAD_DIM:]], axis=1))
        part[u, p] = jnp.dot(
            chooser[u], jnp.concatenate(both, axis=0).astype(BF16),
            preferred_element_type=F32).astype(BF16)

        @pl.when(p != x)
        def _():
            part_copy(u, p).start()

    def rows_z(at):
        return pl.ds(pl.multiple_of(at * z_rows, z_rows), z_rows)

    def half_copy(u, j):
        to = z_at(j)
        return push(half.at[u, rows_z(to)], half_in.at[u, z], rz_s.at[u * ZS + j], rz_r.at[u * ZS + j],
                    x * ZS + to)

    def reduce_x(u):
        total = part[u, x].astype(F32)
        for j in range(1, XS):
            come = part_in.at[u, x_at(-j)]
            push(come, come, rx_r.at[u * XS + j], rx_r.at[u * XS + j], me).wait_recv()
            total += part_in[u, x_at(-j)].astype(F32)
        half[u] = total.astype(BF16)
        for j in NEAREST[::-1]:
            half_copy(u, j).start()

    def project(u):
        attended = half[u, rows_z(z)].astype(F32)
        for j in NEAREST:
            come = half_in.at[u, z_at(-j)]
            push(come, come, rz_r.at[u * ZS + j], rz_r.at[u * ZS + j], me).wait_recv()
            attended += half_in[u, z_at(-j)].astype(F32)
        squares = attended * attended
        sq[u] = (squares[:, :HEAD_DIM] + squares[:, HEAD_DIM:]).reshape(XS, each, HEAD_DIM)
        gate = jnp.concatenate([gate_in[i, u] for i in range(HEADS // XS)], axis=1).astype(F32)
        width = 2 * HEAD_DIM
        gain = gain_attn[:, pl.ds(pl.multiple_of(x * width, width), width)]
        added = jnp.dot(
            (attended * gain * gate).astype(BF16), wo[...], preferred_element_type=F32
        ).reshape(XS, each, HEADS * HEAD_DIM)
        middle = HEADS * HEAD_DIM // 2
        proj[u] = jnp.concatenate([added[:, :, :middle], added[:, :, middle:]], axis=1).astype(BF16)
        for j in (2, 1, 3):
            to = x_at(j)
            send(push(proj.at[u, to], proj_in.at[u, x], po_s.at[u * XS + j], po_r.at[u * XS + j],
                      to * ZS + z))
            send(push(sq.at[u, to], sq_in.at[u, x], sq_s.at[u * XS + j], sq_r.at[u * XS + j],
                      to * ZS + z))

    def finish(u):
        squares = sq[u, x]
        projected = proj[u, x].astype(F32)
        for j in (1, 3, 2):
            frm = x_at(-j)
            push(proj_in.at[u, frm], proj_in.at[u, frm], po_r.at[u * XS + j], po_r.at[u * XS + j],
                 me).wait_recv()
            projected += proj_in[u, frm].astype(F32)
            push(sq_in.at[u, frm], sq_in.at[u, frm], sq_r.at[u * XS + j], sq_r.at[u * XS + j],
                 me).wait_recv()
            squares += sq_in[u, frm]
        scale = lax.rsqrt(
            jnp.sum(squares, axis=1, keepdims=True) * (1.0 / (HEADS * HEAD_DIM)) + EPSILON)
        projected = jnp.concatenate([projected[:each], projected[each:]], axis=1)
        return tokens[u * each : (u + 1) * each] + projected * scale

    def step(k, carry):
        attend(k)

        @pl.when((k == 1) & (gate_x == x))
        def _():
            make_gate()

        @pl.when(k == steps - 2)
        def _():
            reduce_x(0)
            share_wo()

        return carry

    lax.fori_loop(0, steps, step, 0)
    for u in range(1, users):
        reduce_x(u)
    for i in range(HEADS // XS):
        frm = x * (HEADS // XS) + i

        @pl.when(frm != z)
        def _():
            push(gate_in.at[i], gate_in.at[i], ga_r.at[i], ga_r.at[i], me).wait_recv()
    loads[6].wait()
    for j in range(1, team):
        come = wo.at[:, share_of(lax.rem(member - j + team, team))]
        push(come, come, wo_tr.at[j], wo_tr.at[j], me).wait_recv()
    for u in range(users):
        project(u)
    rows_out = [finish(u) for u in range(users)]
    out[...] = jnp.concatenate(rows_out, axis=0).astype(BF16)

    for copy in sends:
        copy.wait_send()
    for j in range(1, team):
        share_copy(j).wait_send()

    @pl.when(gate_x != x)
    def _():
        wg_copy.wait_send()

    @pl.when(gate_x == x)
    def _():
        for j in range(1, ZS):
            gate_copy(j).wait_send()

    for u in range(users):
        for j in range(1, XS):
            part_copy(u, x_at(j)).wait_send()
        for j in range(1, ZS):
            half_copy(u, j).wait_send()


def on_device(
    cand_items, item_rows, hist_keys, hist_values, block_mask, hist_lengths,
    gain_in, w_query, w_gate, gain_attn, w_out,
):
    row_count, users = cand_items.shape
    item_count, width = item_rows.shape
    events = hist_keys.shape[1]
    rows = w_query.shape[0]
    own = row_count * users
    tiles = block_mask.shape[1]
    user_rows = XS * ZS * row_count
    team = min(TEAM, lax.axis_size("users"))
    dma = pltpu.SemaphoreType.DMA
    anywhere = pl.BlockSpec(memory_space=pl.ANY)
    vmem = pl.BlockSpec(memory_space=pltpu.VMEM)
    ranked = pl.pallas_call(
        kernel,
        out_shape=jax.ShapeDtypeStruct((own, width), BF16),
        in_specs=[anywhere] * 11,
        out_specs=vmem,
        scratch_shapes=[
            pltpu.VMEM((users, row_count), jnp.int32),
            pltpu.SMEM(block_mask.shape, jnp.int32),
            pltpu.SMEM((users,), jnp.int32),
            pltpu.VMEM((1, width), F32),
            pltpu.VMEM((1, width), F32),
            pltpu.VMEM((item_count, width), BF16),
            pltpu.VMEM((users, events, width), BF16),
            pltpu.VMEM((users, events, width), BF16),
            pltpu.VMEM((item_count, width), BF16),
            pltpu.VMEM((ZS, own, item_count), BF16),
            pltpu.VMEM((XS, own, ZS * own), BF16),
            pltpu.VMEM((users, user_rows, tiles * item_count), BF16),
            pltpu.VMEM((users * tiles, 1, events), F32),
            pltpu.VMEM((own, width), F32),
            pltpu.VMEM((XS * ZS * rows, HEAD_DIM), BF16),
            pltpu.VMEM((XS, item_count, HEAD_DIM), BF16),
            pltpu.VMEM((XS * ZS * rows, HEAD_DIM), BF16),
            pltpu.VMEM((ZS * rows, width), BF16),
            pltpu.VMEM((HEADS, item_count, HEAD_DIM), BF16),
            pltpu.VMEM((ZS, users, user_rows // ZS, HEAD_DIM), BF16),
            pltpu.VMEM((HEADS // XS, users, user_rows // ZS, HEAD_DIM), BF16),
            pltpu.VMEM((users, XS, user_rows, 2 * HEAD_DIM), BF16),
            pltpu.VMEM((users, XS, user_rows, 2 * HEAD_DIM), BF16),
            pltpu.VMEM((users, user_rows, 2 * HEAD_DIM), BF16),
            pltpu.VMEM((users, ZS, user_rows // ZS, 2 * HEAD_DIM), BF16),
            pltpu.VMEM((users, XS, own, width // 2), BF16),
            pltpu.VMEM((users, XS, own, width // 2), BF16),
            pltpu.VMEM((users, XS, row_count, HEAD_DIM), F32),
            pltpu.VMEM((users, XS, row_count, HEAD_DIM), F32),
            dma((9 + 2 * users,)),
            dma((ZS,)), dma((ZS,)), dma((XS,)), dma((XS,)),
            dma((ZS,)), dma((ZS,)), dma((XS,)), dma((XS,)),
            dma((ZS,)), dma((ZS,)), dma((XS,)), dma((XS,)),
            dma((ZS,)), dma((ZS,)), dma((team,)), dma((team,)),
            dma((ZS,)), dma((ZS,)),
            dma((ZS,)), dma((HEADS // XS,)),
            dma((users * XS,)), dma((users * XS,)),
            dma((users * ZS,)), dma((users * ZS,)),
            dma((users * XS,)), dma((users * XS,)),
            dma((users * XS,)), dma((users * XS,)),
        ],
        compiler_params=pltpu.CompilerParams(
            collective_id=0, has_side_effects=True, vmem_limit_bytes=63 * 1024 * 1024),
        cost_estimate=pl.CostEstimate(flops=10**9, bytes_accessed=5 * 10**6, transcendentals=10**6),
        name="ranked",
    )(
        cand_items.T, item_rows, hist_keys, hist_values, block_mask, hist_lengths,
        gain_in.reshape(1, width), w_query, w_gate, gain_attn.reshape(1, width), w_out,
    )
    return ranked.reshape(users, row_count, width).transpose(1, 0, 2)


def solution(mesh):
    in_specs = (
        P(("users", "seq"), None),
        P("users", None),
        P("users", "seq", None),
        P("users", "seq", None),
        P("users", None, "seq"),
        P("users"),
        P(),
        P("seq", None),
        P("seq", None),
        P(),
        P("seq", None),
    )
    out_specs = P(("users", "seq"), None, None)
    return jax.shard_map(
        on_device, mesh=mesh, in_specs=in_specs, out_specs=out_specs, check_vma=False
    )
```

```python
import jax
import jax.numpy as jnp
from jax import lax
from jax.experimental import pallas as pl
from jax.experimental.pallas import tpu as pltpu
from jax.sharding import PartitionSpec as P

HEADS = 8
HEAD_DIM = 128
BLOCK = 128
EPSILON = 1e-06
XS, ZS = 4, 8
NEAREST = (7, 1, 6, 2, 5, 3, 4)
TEAM = 4
MESH = pl.DeviceIdType.MESH
BF16, F32 = jnp.bfloat16, jnp.float32


def silu(v):
    return v / (1.0 + jnp.exp(-v))


def push(src, dst, send_sem, recv_sem, seq):
    return pltpu.make_async_remote_copy(
        src_ref=src, dst_ref=dst, send_sem=send_sem, recv_sem=recv_sem,
        device_id={"seq": seq}, device_id_type=MESH)


def kernel(
    cand_hbm, items_hbm, keys_hbm, vals_hbm, mask_hbm, lens_hbm, gain_in_hbm, wq_hbm, wg_hbm,
    gain_attn_hbm, wo_hbm,
    out,
    cand, mask, lens, gain_in, gain_attn, items, keys, vals, normed, picks, ids_x, chooser, live,
    tokens, wq, query_part, wg, wo, query, gate_out, gate_in, part, part_in, half, half_in, proj, proj_in, sq, sq_in,
    load_sem, wq_zs, wq_zr, wq_xs, wq_xr, wg_zs, wg_zr, wg_xs, wg_xr, oh_zs, oh_zr, oh_xs, oh_xr,
    wo_zs, wo_zr, wo_ts, wo_tr, q_s, q_r, ga_s, ga_r, rx_s, rx_r, rz_s, rz_r, po_s, po_r, sq_s, sq_r,
):
    me = lax.axis_index("seq")
    x, z = lax.div(me, ZS), lax.rem(me, ZS)
    team = min(TEAM, lax.axis_size("users"))
    member = lax.rem(lax.axis_index("users"), team)
    team_at = lax.axis_index("users") - member
    rows = wq_hbm.shape[0]
    own = picks.shape[1]
    tiles = mask.shape[1]
    users, events = keys_hbm.shape[0], keys_hbm.shape[1]
    item_count = items_hbm.shape[0]

    def z_at(step):
        return lax.rem(z + step + ZS, ZS)

    def x_at(step):
        return lax.rem(x + step + XS, XS)

    def lanes(index):
        return pl.ds(pl.multiple_of(index * HEAD_DIM, HEAD_DIM), HEAD_DIM)

    def rows_of(seq):
        return pl.ds(pl.multiple_of(seq * rows, rows), rows)

    share = wo_hbm.shape[1] // team

    def share_of(at):
        return pl.ds(pl.multiple_of(at * share, share), share)

    def mate(step):
        return lax.rem(member + step, team)

    barrier = pltpu.get_barrier_semaphore()
    for j in range(1, ZS):
        pl.semaphore_signal(barrier, inc=1, device_id={"seq": x * ZS + z_at(j)}, device_id_type=MESH)
    for j in range(1, XS):
        pl.semaphore_signal(barrier, inc=1, device_id={"seq": x_at(j) * ZS + z}, device_id_type=MESH)

    for j in range(1, team):
        pl.semaphore_signal(barrier, inc=1, device_id={"users": team_at + mate(j)}, device_id_type=MESH)

    loads = [
        pltpu.make_async_copy(cand_hbm, cand, load_sem.at[0]),
        pltpu.make_async_copy(items_hbm, items, load_sem.at[1]),
        pltpu.make_async_copy(gain_in_hbm, gain_in, load_sem.at[2]),
        pltpu.make_async_copy(wq_hbm.at[:, lanes(z)], wq.at[rows_of(me)], load_sem.at[3]),
        pltpu.make_async_copy(wg_hbm.at[:, lanes(z)], wg.at[rows_of(me)], load_sem.at[4]),
        pltpu.make_async_copy(
            wo_hbm.at[:, share_of(member)], wo.at[rows_of(z), share_of(member)], load_sem.at[5]),
        pltpu.make_async_copy(gain_attn_hbm, gain_attn, load_sem.at[6]),
        pltpu.make_async_copy(mask_hbm, mask, load_sem.at[7]),
        pltpu.make_async_copy(lens_hbm, lens, load_sem.at[8]),
    ]
    for u in range(users):
        loads.append(pltpu.make_async_copy(keys_hbm.at[u], keys.at[u], load_sem.at[9 + 2 * u]))
        loads.append(pltpu.make_async_copy(vals_hbm.at[u], vals.at[u], load_sem.at[10 + 2 * u]))
    for load in loads[:4]:
        load.start()

    pl.semaphore_wait(barrier, XS + ZS + team - 3)

    sends = []

    def send(copy):
        copy.start()
        sends.append(copy)

    for j in range(1, ZS):
        to = z_at(j)
        send(push(wq_hbm.at[:, lanes(to)], wq.at[rows_of(me)], wq_zs.at[j], wq_zr.at[j], x * ZS + to))
    for load in loads[4:]:
        load.start()

    loads[0].wait()
    each = own // users
    row = lax.broadcasted_iota(jnp.int32, (own, each), 0)
    column = lax.broadcasted_iota(jnp.int32, (own, each), 1)
    ids = jnp.zeros((own, 1), F32)
    for u in range(users):
        here = row == column + u * each
        ids += jnp.sum(
            jnp.where(here, cand[u : u + 1, :].astype(F32), 0.0), axis=1, keepdims=True)
    item = lax.broadcasted_iota(jnp.int32, (own, item_count), 1).astype(F32)
    own_pick = jnp.where(item == ids, 1.0, 0.0).astype(BF16)
    picks[z] = own_pick

    for j in range(1, ZS):
        send(push(picks.at[z], picks.at[z], oh_zs.at[j], oh_zr.at[j], x * ZS + z_at(j)))

    loads[1].wait()
    loads[2].wait()
    wide = items[...].astype(F32)
    normed[...] = (
        wide * lax.rsqrt(jnp.mean(wide * wide, axis=-1, keepdims=True) + EPSILON) * gain_in[...]
    ).astype(BF16)

    def group(at):
        return pl.ds(pl.multiple_of(at * (ZS * rows), ZS * rows), ZS * rows)

    loads[3].wait()
    for j in range(1, ZS):
        come = wq.at[rows_of(x * ZS + z_at(-j))]
        push(come, come, wq_zr.at[j], wq_zr.at[j], me).wait_recv()
    depth = ZS * rows
    own_part = jnp.dot(
        normed[:, pl.ds(pl.multiple_of(x * depth, depth), depth)], wq[group(x)],
        preferred_element_type=F32)
    query_part[x] = own_part.astype(BF16)
    for j in range(1, XS):
        send(push(query_part.at[x], query_part.at[x], wq_xs.at[j], wq_xr.at[j], x_at(j) * ZS + z))

    for j in range(1, ZS):
        to = z_at(j)
        send(push(wg_hbm.at[:, lanes(to)], wg.at[rows_of(me)], wg_zs.at[j], wg_zr.at[j], x * ZS + to))

    for j in range(1, ZS):
        come = picks.at[z_at(-j)]
        push(come, come, oh_zr.at[j], oh_zr.at[j], me).wait_recv()
    group_rows = ZS * own
    picked = picks[...].reshape(group_rows, item_count)
    number = lax.broadcasted_iota(jnp.int32, (own, item_count), 1).astype(F32).astype(BF16)
    ids_x[x] = lax.dot_general(
        number, picked, (((1,), (1,)), ((), ())), preferred_element_type=F32).astype(BF16)
    for j in range(1, XS):
        send(push(ids_x.at[x], ids_x.at[x], oh_xs.at[j], oh_xr.at[j], x_at(j) * ZS + z))

    tokens[...] = jnp.dot(own_pick, items[...], preferred_element_type=F32)
    loads[7].wait()
    loads[8].wait()
    for u in range(users):
        length = lens[u] - me * events
        for t in range(tiles):
            for b in range(events // BLOCK):
                place = b * BLOCK + lax.broadcasted_iota(jnp.int32, (1, BLOCK), 1)
                opened = jnp.full((1, BLOCK), mask[u, t, b], jnp.int32)
                live[u * tiles + t, :, pl.ds(b * BLOCK, BLOCK)] = jnp.where(
                    (opened == 1) & (place < length), 1.0, 0.0)

    asked_z = own_part
    for j in range(1, XS):
        come = query_part.at[x_at(-j)]
        push(come, come, wq_xr.at[j], wq_xr.at[j], me).wait_recv()
        asked_z += query_part[x_at(-j)].astype(F32)
    query[z] = silu(asked_z).astype(BF16)
    for j in NEAREST:
        send(push(query.at[z], query.at[z], q_s.at[j], q_r.at[j], x * ZS + z_at(j)))

    gate_x = lax.div(z, HEADS // XS)
    gate_step = lax.rem(gate_x - x + XS, XS)
    wg_copy = push(wg.at[group(x)], wg.at[group(x)], wg_xs.at[gate_step], wg_xr.at[gate_step],
                   gate_x * ZS + z)
    slot = lax.rem(z, HEADS // XS)
    loads[4].wait()
    for j in range(1, ZS):
        come = wg.at[rows_of(x * ZS + z_at(-j))]
        push(come, come, wg_zr.at[j], wg_zr.at[j], me).wait_recv()

    @pl.when(gate_x != x)
    def _():
        wg_copy.start()

    for j in range(1, ZS):
        send(push(wo_hbm.at[:, share_of(member)], wo.at[rows_of(z), share_of(member)],
                  wo_zs.at[j], wo_zr.at[j], x * ZS + z_at(j)))

    def share_copy(j):
        return pltpu.make_async_remote_copy(
            src_ref=wo.at[:, share_of(member)], dst_ref=wo.at[:, share_of(member)],
            send_sem=wo_ts.at[j], recv_sem=wo_tr.at[j],
            device_id={"users": team_at + mate(j)}, device_id_type=MESH)

    def share_wo():
        loads[5].wait()
        for j in range(1, ZS):
            come = wo.at[rows_of(z_at(-j)), share_of(member)]
            push(come, come, wo_zr.at[j], wo_zr.at[j], me).wait_recv()
        for j in range(1, team):
            share_copy(j).start()

    for j in range(1, XS):
        come = ids_x.at[x_at(-j)]
        push(come, come, oh_xr.at[j], oh_xr.at[j], me).wait_recv()
    down = lax.broadcasted_iota(jnp.int32, (item_count, group_rows), 0).astype(F32)
    per_tile = XS // tiles
    user_rows = XS * ZS * each
    z_rows = XS * each
    shown = []
    for s in range(XS):
        chosen = jnp.transpose(jnp.where(down == ids_x[s, 0:1, :].astype(F32), 1.0, 0.0))
        shown.append(chosen.reshape(ZS, own, item_count))
    blank = jnp.zeros((ZS, each, item_count), F32)
    for u in range(users):
        wide_rows = []
        for s in range(XS):
            mine = shown[s][:, u * each : (u + 1) * each]
            wide_rows.append(jnp.concatenate(
                [mine if t == s // per_tile else blank for t in range(tiles)], axis=2))
        chooser[u] = jnp.concatenate(wide_rows, axis=1).reshape(
            user_rows, tiles * item_count).astype(BF16)

    def gate_copy(j):
        to = z_at(j)
        return push(gate_out.at[to], gate_in.at[slot], ga_s.at[j], ga_r.at[slot], x * ZS + to)

    def make_gate():
        for j in range(1, XS):
            come = wg.at[group(x_at(-j))]
            push(come, come, wg_xr.at[j], wg_xr.at[j], me).wait_recv()
        gate_items = silu(jnp.dot(normed[...], wg[...], preferred_element_type=F32)).astype(BF16)
        twice = jnp.concatenate([gate_items] * tiles, axis=0)
        for u in range(users):
            gate_out[:, u] = jnp.dot(
                chooser[u], twice, preferred_element_type=F32
            ).astype(BF16).reshape(ZS, z_rows, HEAD_DIM)
        for j in NEAREST[::-1]:
            gate_copy(j).start()
        gate_in[slot] = gate_out[z]

    for load in loads[9:]:
        load.wait()

    pairs = HEADS // 2
    steps = users * pairs

    def place_of(k):
        u, s = lax.div(k, pairs), lax.rem(k, pairs)
        early = lax.div(z, 2) + s + lax.div(s, 2) * (5 - 2 * s)
        late = x + 1 + s
        first = jnp.where(u == 0, 1, 0)
        return u, lax.rem(first * early + (1 - first) * late + 2 * pairs, pairs)

    def part_copy(u, p):
        j = lax.rem(p - x + XS, XS)
        return push(part.at[u, p], part_in.at[u, x], rx_s.at[u * XS + j], rx_r.at[u * XS + j],
                    p * ZS + z)

    def attend(k):
        u, p = place_of(k)
        heads = (2 * p, 2 * p + 1)

        for h in heads:
            @pl.when((k < pairs) & (h != z))
            def _():
                j = lax.rem(z - h + ZS, ZS)
                push(query.at[h], query.at[h], q_r.at[j], q_r.at[j], me).wait_recv()

        nothing = jnp.zeros((item_count, HEAD_DIM), BF16)
        asked = jnp.concatenate([
            jnp.concatenate([query[heads[0]], nothing], axis=1),
            jnp.concatenate([nothing, query[heads[1]]], axis=1)], axis=0)
        columns = pl.ds(pl.multiple_of(p * 2 * HEAD_DIM, 2 * HEAD_DIM), 2 * HEAD_DIM)
        scores = lax.dot_general(
            asked, keys[u, :, columns], (((1,), (1,)), ((), ())), preferred_element_type=F32)
        halved = scores * (0.5 * HEAD_DIM ** (-0.5))
        weight = halved + halved * jnp.tanh(halved)
        kept = jnp.concatenate(
            [(weight * live[u * tiles + t]).astype(BF16) for t in range(tiles)], axis=0)
        sums = jnp.dot(kept, vals[u, :, columns], preferred_element_type=F32)
        both = []
        for t in range(tiles):
            at = t * 2 * item_count
            both.append(jnp.concatenate([
                sums[at : at + item_count, :HEAD_DIM],
                sums[at + item_count : at + 2 * item_count, HEAD_DIM:]], axis=1))
        part[u, p] = jnp.dot(
            chooser[u], jnp.concatenate(both, axis=0).astype(BF16),
            preferred_element_type=F32).astype(BF16)

        @pl.when(p != x)
        def _():
            part_copy(u, p).start()

    def rows_z(at):
        return pl.ds(pl.multiple_of(at * z_rows, z_rows), z_rows)

    def half_copy(u, j):
        to = z_at(j)
        return push(half.at[u, rows_z(to)], half_in.at[u, z], rz_s.at[u * ZS + j], rz_r.at[u * ZS + j],
                    x * ZS + to)

    def reduce_x(u):
        total = part[u, x].astype(F32)
        for j in range(1, XS):
            come = part_in.at[u, x_at(-j)]
            push(come, come, rx_r.at[u * XS + j], rx_r.at[u * XS + j], me).wait_recv()
            total += part_in[u, x_at(-j)].astype(F32)
        half[u] = total.astype(BF16)
        for j in NEAREST[::-1]:
            half_copy(u, j).start()

    def project(u):
        attended = half[u, rows_z(z)].astype(F32)
        for j in NEAREST:
            come = half_in.at[u, z_at(-j)]
            push(come, come, rz_r.at[u * ZS + j], rz_r.at[u * ZS + j], me).wait_recv()
            attended += half_in[u, z_at(-j)].astype(F32)
        squares = attended * attended
        sq[u] = (squares[:, :HEAD_DIM] + squares[:, HEAD_DIM:]).reshape(XS, each, HEAD_DIM)
        gate = jnp.concatenate([gate_in[i, u] for i in range(HEADS // XS)], axis=1).astype(F32)
        width = 2 * HEAD_DIM
        gain = gain_attn[:, pl.ds(pl.multiple_of(x * width, width), width)]
        added = jnp.dot(
            (attended * gain * gate).astype(BF16), wo[...], preferred_element_type=F32
        ).reshape(XS, each, HEADS * HEAD_DIM)
        middle = HEADS * HEAD_DIM // 2
        proj[u] = jnp.concatenate([added[:, :, :middle], added[:, :, middle:]], axis=1).astype(BF16)
        for j in (2, 1, 3):
            to = x_at(j)
            send(push(proj.at[u, to], proj_in.at[u, x], po_s.at[u * XS + j], po_r.at[u * XS + j],
                      to * ZS + z))
            send(push(sq.at[u, to], sq_in.at[u, x], sq_s.at[u * XS + j], sq_r.at[u * XS + j],
                      to * ZS + z))

    def finish(u):
        squares = sq[u, x]
        projected = proj[u, x].astype(F32)
        for j in (1, 3, 2):
            frm = x_at(-j)
            push(proj_in.at[u, frm], proj_in.at[u, frm], po_r.at[u * XS + j], po_r.at[u * XS + j],
                 me).wait_recv()
            projected += proj_in[u, frm].astype(F32)
            push(sq_in.at[u, frm], sq_in.at[u, frm], sq_r.at[u * XS + j], sq_r.at[u * XS + j],
                 me).wait_recv()
            squares += sq_in[u, frm]
        scale = lax.rsqrt(
            jnp.sum(squares, axis=1, keepdims=True) * (1.0 / (HEADS * HEAD_DIM)) + EPSILON)
        projected = jnp.concatenate([projected[:each], projected[each:]], axis=1)
        return tokens[u * each : (u + 1) * each] + projected * scale

    def step(k, carry):
        attend(k)

        @pl.when((k == 1) & (gate_x == x))
        def _():
            make_gate()

        @pl.when(k == steps - 2)
        def _():
            reduce_x(0)
            share_wo()

        return carry

    lax.fori_loop(0, steps, step, 0)
    for u in range(1, users):
        reduce_x(u)
    for i in range(HEADS // XS):
        frm = x * (HEADS // XS) + i

        @pl.when(frm != z)
        def _():
            push(gate_in.at[i], gate_in.at[i], ga_r.at[i], ga_r.at[i], me).wait_recv()
    loads[6].wait()
    for j in range(1, team):
        come = wo.at[:, share_of(lax.rem(member - j + team, team))]
        push(come, come, wo_tr.at[j], wo_tr.at[j], me).wait_recv()
    rows_out = []
    for u in range(users):
        project(u)
        rows_out.append(finish(u))
    out[...] = jnp.concatenate(rows_out, axis=0).astype(BF16)

    for copy in sends:
        copy.wait_send()
    for j in range(1, team):
        share_copy(j).wait_send()

    @pl.when(gate_x != x)
    def _():
        wg_copy.wait_send()

    @pl.when(gate_x == x)
    def _():
        for j in range(1, ZS):
            gate_copy(j).wait_send()

    for u in range(users):
        for j in range(1, XS):
            part_copy(u, x_at(j)).wait_send()
        for j in range(1, ZS):
            half_copy(u, j).wait_send()


def on_device(
    cand_items, item_rows, hist_keys, hist_values, block_mask, hist_lengths,
    gain_in, w_query, w_gate, gain_attn, w_out,
):
    row_count, users = cand_items.shape
    item_count, width = item_rows.shape
    events = hist_keys.shape[1]
    rows = w_query.shape[0]
    own = row_count * users
    tiles = block_mask.shape[1]
    user_rows = XS * ZS * row_count
    team = min(TEAM, lax.axis_size("users"))
    dma = pltpu.SemaphoreType.DMA
    anywhere = pl.BlockSpec(memory_space=pl.ANY)
    vmem = pl.BlockSpec(memory_space=pltpu.VMEM)
    ranked = pl.pallas_call(
        kernel,
        out_shape=jax.ShapeDtypeStruct((own, width), BF16),
        in_specs=[anywhere] * 11,
        out_specs=vmem,
        scratch_shapes=[
            pltpu.VMEM((users, row_count), jnp.int32),
            pltpu.SMEM(block_mask.shape, jnp.int32),
            pltpu.SMEM((users,), jnp.int32),
            pltpu.VMEM((1, width), F32),
            pltpu.VMEM((1, width), F32),
            pltpu.VMEM((item_count, width), BF16),
            pltpu.VMEM((users, events, width), BF16),
            pltpu.VMEM((users, events, width), BF16),
            pltpu.VMEM((item_count, width), BF16),
            pltpu.VMEM((ZS, own, item_count), BF16),
            pltpu.VMEM((XS, own, ZS * own), BF16),
            pltpu.VMEM((users, user_rows, tiles * item_count), BF16),
            pltpu.VMEM((users * tiles, 1, events), F32),
            pltpu.VMEM((own, width), F32),
            pltpu.VMEM((XS * ZS * rows, HEAD_DIM), BF16),
            pltpu.VMEM((XS, item_count, HEAD_DIM), BF16),
            pltpu.VMEM((XS * ZS * rows, HEAD_DIM), BF16),
            pltpu.VMEM((ZS * rows, width), BF16),
            pltpu.VMEM((HEADS, item_count, HEAD_DIM), BF16),
            pltpu.VMEM((ZS, users, user_rows // ZS, HEAD_DIM), BF16),
            pltpu.VMEM((HEADS // XS, users, user_rows // ZS, HEAD_DIM), BF16),
            pltpu.VMEM((users, XS, user_rows, 2 * HEAD_DIM), BF16),
            pltpu.VMEM((users, XS, user_rows, 2 * HEAD_DIM), BF16),
            pltpu.VMEM((users, user_rows, 2 * HEAD_DIM), BF16),
            pltpu.VMEM((users, ZS, user_rows // ZS, 2 * HEAD_DIM), BF16),
            pltpu.VMEM((users, XS, own, width // 2), BF16),
            pltpu.VMEM((users, XS, own, width // 2), BF16),
            pltpu.VMEM((users, XS, row_count, HEAD_DIM), F32),
            pltpu.VMEM((users, XS, row_count, HEAD_DIM), F32),
            dma((9 + 2 * users,)),
            dma((ZS,)), dma((ZS,)), dma((XS,)), dma((XS,)),
            dma((ZS,)), dma((ZS,)), dma((XS,)), dma((XS,)),
            dma((ZS,)), dma((ZS,)), dma((XS,)), dma((XS,)),
            dma((ZS,)), dma((ZS,)), dma((team,)), dma((team,)),
            dma((ZS,)), dma((ZS,)),
            dma((ZS,)), dma((HEADS // XS,)),
            dma((users * XS,)), dma((users * XS,)),
            dma((users * ZS,)), dma((users * ZS,)),
            dma((users * XS,)), dma((users * XS,)),
            dma((users * XS,)), dma((users * XS,)),
        ],
        compiler_params=pltpu.CompilerParams(
            collective_id=0, has_side_effects=True, vmem_limit_bytes=63 * 1024 * 1024),
        cost_estimate=pl.CostEstimate(flops=10**9, bytes_accessed=5 * 10**6, transcendentals=10**6),
        name="ranked",
    )(
        cand_items.T, item_rows, hist_keys, hist_values, block_mask, hist_lengths,
        gain_in.reshape(1, width), w_query, w_gate, gain_attn.reshape(1, width), w_out,
    )
    return ranked.reshape(users, row_count, width).transpose(1, 0, 2)


def solution(mesh):
    in_specs = (
        P(("users", "seq"), None),
        P("users", None),
        P("users", "seq", None),
        P("users", "seq", None),
        P("users", None, "seq"),
        P("users"),
        P(),
        P("seq", None),
        P("seq", None),
        P(),
        P("seq", None),
    )
    out_specs = P(("users", "seq"), None, None)
    return jax.shard_map(
        on_device, mesh=mesh, in_specs=in_specs, out_specs=out_specs, check_vma=False
    )
```
